32 devices in a mesh: groups: 2 (over y), dp: 8 (over z, x), tensor: 2 (over core).
Axes of the slice: x: 2, y: 2, z: 4, core: 2. Of those that a mesh axis runs over, the one named last changes fastest.
Arguments:
- tokens: bfloat16 [4096, 5120], P(('groups', 'dp'), 'tensor'), parts along dimension 0, may hold values from -60 to 60
- base_key_matrix: bfloat16 [5120, 1024], P('tensor'), may hold values from -0.078125 to 0.078125
- adapter_down_weight: bfloat16 [256, 64, 5120], P(('groups', 'dp'), None, 'tensor'), parts along dimension 0, may hold values from -0.078125 to 0.078125
- adapter_up_weight: bfloat16 [256, 64, 1024], P(('groups', 'dp'), None, 'tensor'), parts along dimension 0, may hold values from -0.75 to 0.75
- key_norm_scale: float32 [128], replicated, may hold values from 0.25 to 1.75
- request_adapter: int32 [4096], P(('groups', 'dp')), parts along dimension 0, may hold values from 0 to 127, as said below
- adapter_slot_table: int32 [256], P('groups'), parts along dimension 0, may hold values from 0 to 127, as said below
- cached_token_length: int32 [4096], P(('groups', 'dp')), parts along dimension 0, may hold values from 1 to 4096
Outputs:
- new_keys: bfloat16 [4096, 1024], P(('groups', 'dp'), 'tensor'), parts along dimension 0
The draws below stay inside these ranges and needn't reach their ends.
There are 2 independent parts, one for each index of `groups`. The reference program is written for one: setup_inputs(seed, part) draws one part's arguments, and reference() takes and returns one part's arrays. A program takes and returns all parts, laid end to end along the dimension named above; an argument that names none is the same for every part. Nothing has to cross between parts.
Inputs may be any that keep to these rules, and one draw needn't show every extreme that they name: `request_adapter`: in the 256 requests of each index of dp, exactly 96 use adapters stored on one owner (slot // 16), the same owner for every index and every request block of the part, and every other owner gets 23 or 22 of them. A permutation: adapter a is row adapter_slot_table[a] of adapter_down_weight and adapter_up_weight.
All inputs are finite; a program needn't handle non-finite values.
Results may differ from the reference program's by a relative error of at most 0.0051.
Values may be sent and summed in bfloat16 or wider, within the bound.
No kernel may reach another device: no remote copies, remote signals or barrier semaphores. Data moves between devices by JAX's collectives and lax.ppermute only.
A program may use at most 128 MiB of HBM per device.

```python
import math
import jax
import jax.numpy as jnp
from jax import lax

MODEL_WIDTH = 5120
KV_HEADS = 8
HEAD = 128
ADAPTER_RANK = 64
ADAPT_DEV = 16
TOK_DEV = 256
KEY_FEATURES = 1024
ADAPTER_TOTAL = 128
TOKENS = 2048
CAP = 96
N_DP = 8


def block_order(order_key):
    return jax.random.permutation(order_key, TOK_DEV)


def common_routes(key):
    perm_key, hot_key, order_key, local_key = jax.random.split(key, 4)
    placed = jax.random.permutation(perm_key, ADAPTER_TOTAL).astype(jnp.int32)
    hot_owner = jax.random.randint(hot_key, (), 0, N_DP)
    orders = jax.vmap(block_order)(jax.random.split(order_key, N_DP)).astype(jnp.int32)
    beyond = orders - CAP
    others = (hot_owner + 1 + jnp.maximum(beyond, 0) % (N_DP - 1)) % N_DP
    owner_of = jnp.where(orders < CAP, hot_owner, others)
    local_idx = jax.random.randint(local_key, (N_DP, TOK_DEV), 0, ADAPT_DEV)
    chosen = jnp.take(placed, owner_of * ADAPT_DEV + local_idx)
    return (placed, chosen.reshape(TOKENS).astype(jnp.int32))


def draw_request_adapter(key, part):
    placed, chosen = common_routes(key)
    return chosen


def draw_adapter_slot_table(key, part):
    placed, chosen = common_routes(key)
    return jnp.argsort(placed).astype(jnp.int32)


def draw_tokens(key, part):
    key = jax.random.fold_in(key, 7)
    value_key, row_key, column_key = jax.random.split(key, 3)
    row_scale = jnp.exp(jax.random.uniform(row_key, (TOKENS, 1), jnp.float32, jnp.log(0.3), jnp.log(3.0)))
    column_scale = jnp.exp(jax.random.uniform(column_key, (1, MODEL_WIDTH), jnp.float32, jnp.log(0.3), jnp.log(3.0)))
    values = jnp.clip(jax.random.normal(value_key, (TOKENS, MODEL_WIDTH), jnp.float32), -6.0, 6.0)
    return (values * row_scale * column_scale).astype(jnp.bfloat16)


def with_ends(array, key, smallest, high):
    place = [jax.random.randint(jax.random.fold_in(key, axis), (), 0, length) for axis, length in enumerate(array.shape)]
    longest = array.shape.index(max(array.shape))
    neighbour = place[:longest] + [(place[longest] + 1) % array.shape[longest]] + place[longest + 1:]
    return array.at[tuple(place)].set(smallest).at[tuple(neighbour)].set(high)


def shard_levels(own_key, shape, cuts, least, largest):
    def one(dim, parts):
        steps = jax.random.uniform(jax.random.fold_in(jax.random.fold_in(own_key, 6), dim), (parts,), jnp.float32, least / len(cuts), largest / len(cuts))
        return jnp.repeat(jnp.exp(steps), shape[dim] // parts).reshape((-1,) + (1,) * (len(shape) - dim - 1))

    loudness = one(*cuts[0])
    for cut in cuts[1:]:
        loudness = loudness * one(*cut)
    return loudness


def gaussian(key, extent, scale, limit, cuts=(), kind=jnp.bfloat16):
    result = scale * jax.random.normal(key, extent, jnp.float32)
    if cuts:
        result = result * shard_levels(key, extent, cuts, -0.22, 0.18)
    return jnp.clip(result, -limit, limit).astype(kind)


def setup_inputs(seed: int = 0, part: int = 0) -> dict:
    streams_of = jax.random.split(jax.random.key(seed), 9)
    part_keys = jax.random.split(jax.random.fold_in(streams_of[8], part), 9)
    tokens = draw_tokens(jax.random.fold_in(jax.random.fold_in(streams_of[8], part), 71), part)
    base_key_matrix = gaussian(streams_of[1], (MODEL_WIDTH, KEY_FEATURES), MODEL_WIDTH ** -0.5, 0.078125, ((0, 2),))
    adapter_down_weight = gaussian(part_keys[2], (ADAPTER_TOTAL, ADAPTER_RANK, MODEL_WIDTH), MODEL_WIDTH ** -0.5, 0.078125, ((0, 8), (2, 2)))
    adapter_up_weight = gaussian(part_keys[3], (ADAPTER_TOTAL, ADAPTER_RANK, KEY_FEATURES), ADAPTER_RANK ** -0.5, 0.75, ((0, 8), (2, 2)))
    key_norm_scale = jnp.clip(1.0 + 0.15 * jax.random.normal(streams_of[4], (HEAD,), jnp.float32), 0.25, 1.75)
    request_adapter = draw_request_adapter(jax.random.fold_in(jax.random.fold_in(streams_of[8], part), 71), part)
    adapter_slot_table = draw_adapter_slot_table(jax.random.fold_in(jax.random.fold_in(streams_of[8], part), 71), part)
    cached_token_length = with_ends(jax.random.randint(part_keys[7], (TOKENS,), 1, 4097), jax.random.fold_in(part_keys[7], 1), 1, 4096).astype(jnp.int32)
    return {"tokens": tokens, "base_key_matrix": base_key_matrix, "adapter_down_weight": adapter_down_weight, "adapter_up_weight": adapter_up_weight, "key_norm_scale": key_norm_scale, "request_adapter": request_adapter, "adapter_slot_table": adapter_slot_table, "cached_token_length": cached_token_length}


rope_theta = 1000000.0

def rotate(normed, cached_token_length):
    head_size = normed.shape[-1]
    half_head = head_size // 2
    inv_freq = rope_theta ** (-(jnp.arange(half_head, dtype=jnp.float32) * 2.0) / head_size)
    angles = cached_token_length.astype(jnp.float32)[:, None] * inv_freq[None, :]
    cosine = jnp.cos(angles)[:, None, :]
    sine = jnp.sin(angles)[:, None, :]
    lead_half = normed[..., :half_head]
    tail_half = normed[..., half_head:]
    return jnp.concatenate([lead_half * cosine - tail_half * sine, tail_half * cosine + lead_half * sine], axis=-1)

def reference(tokens, base_key_matrix, adapter_down_weight, adapter_up_weight, key_norm_scale, request_adapter, adapter_slot_table, cached_token_length):
    base = jnp.dot(tokens, base_key_matrix, preferred_element_type=jnp.float32)
    slot_idx = jnp.take(adapter_slot_table, request_adapter).astype(jnp.int32)
    block_rows = math.gcd(TOKENS, 128)
    block_count = TOKENS // block_rows

    def one_block(pieces):
        token_block, storage_slot_block = pieces
        down_weight_rows = jnp.take(adapter_down_weight, storage_slot_block, axis=0).astype(jnp.float32)
        reduced_input = jnp.einsum('nd,nrd->nr', token_block.astype(jnp.float32), down_weight_rows, precision=lax.Precision.HIGHEST)
        reduced_input = reduced_input.astype(jnp.bfloat16)
        up_weight_rows = jnp.take(adapter_up_weight, storage_slot_block, axis=0).astype(jnp.float32)
        expanded_delta = jnp.einsum('nr,nrk->nk', reduced_input.astype(jnp.float32), up_weight_rows, precision=lax.Precision.HIGHEST)
        return expanded_delta.astype(jnp.bfloat16)
    delta_rows = lax.map(one_block, (tokens.reshape(block_count, block_rows, MODEL_WIDTH), slot_idx.reshape(block_count, block_rows)))
    delta_rows = delta_rows.reshape(TOKENS, KEY_FEATURES)
    key_vals = base + delta_rows.astype(jnp.float32)
    head_view = key_vals.reshape(TOKENS, KV_HEADS, HEAD)
    normed = head_view * lax.rsqrt(lax.optimization_barrier(jnp.mean(head_view * head_view, axis=-1, keepdims=True)) + 1e-06) * key_norm_scale
    rotated = rotate(normed, cached_token_length)
    return rotated.reshape(TOKENS, KEY_FEATURES).astype(jnp.bfloat16)
```

```python
import functools

import jax
import jax.numpy as jnp
from jax import lax
from jax.experimental import pallas as pl
from jax.experimental.pallas import tpu as pltpu
from jax.sharding import PartitionSpec as P

rope_theta = 1000000.0
LANES = 128
EXTRA = 128
HOT_PARTS = 3
VMEM_BYTES = 48 * 1024 * 1024


def whole():
    return pl.BlockSpec(memory_space=pltpu.VMEM)


def params():
    return pltpu.CompilerParams(vmem_limit_bytes=VMEM_BYTES)


def ring_order(owners):
    return [i for i in range(0, owners, 2)] + [i for i in range(owners - 1, 0, -2)]


def to_column(row):
    count = row.shape[1]
    square = lax.broadcasted_iota(jnp.int32, (count, count), 0) == lax.broadcasted_iota(
        jnp.int32, (count, count), 1
    )
    return jnp.sum(jnp.where(square, row, 0), axis=1, keepdims=True)


def pack_kernel(
    stored, owners, share, request_ref, table_ref, tokens_ref, cold_ref, hot_ref, place_ref
):
    count = request_ref.shape[1]
    width = tokens_ref.shape[1]
    request_col = to_column(request_ref[...])
    adapters = table_ref.shape[1]
    match = request_col == lax.broadcasted_iota(jnp.int32, (count, adapters), 1)
    slot_col = jnp.sum(jnp.where(match, table_ref[...], 0), axis=1, keepdims=True)
    row_id = lax.broadcasted_iota(jnp.int32, (count, count), 0)
    col_id = lax.broadcasted_iota(jnp.int32, (count, count), 1)
    slot_row = jnp.sum(jnp.where(row_id == col_id, slot_col, 0), axis=0, keepdims=True)
    owner_col = slot_col // stored
    owner_row = slot_row // stored
    same = owner_col == owner_row
    rank_col = jnp.sum(jnp.where(same & (col_id < row_id), 1, 0), axis=1, keepdims=True)
    rank_row = jnp.sum(jnp.where(same & (row_id < col_id), 1, 0), axis=0, keepdims=True)
    cold_total = owners * share
    hot_total = HOT_PARTS * share

    def place(owner, rank):
        return jnp.where(rank < share, owner * share + rank, cold_total + rank - share)

    place_ref[...] = place(owner_col, rank_col)
    place_row = place(owner_row, rank_row)
    local_row = slot_row - owner_row * stored
    cold_pick = place_row == lax.broadcasted_iota(jnp.int32, (cold_total, count), 0)
    hot_pick = place_row - cold_total == lax.broadcasted_iota(jnp.int32, (hot_total, count), 0)
    tokens = tokens_ref[...]
    cold_ref[:, :width] = jnp.dot(
        cold_pick.astype(jnp.float32).astype(jnp.bfloat16), tokens, preferred_element_type=jnp.float32
    ).astype(jnp.bfloat16)
    hot_ref[...] = jnp.dot(
        hot_pick.astype(jnp.float32).astype(jnp.bfloat16), tokens, preferred_element_type=jnp.float32
    ).astype(jnp.bfloat16)
    lane = lax.broadcasted_iota(jnp.int32, (cold_total, EXTRA), 1)
    part_row = lax.broadcasted_iota(jnp.int32, (cold_total, count), 0) % share
    extra = jnp.sum(jnp.where(cold_pick, local_row + 1, 0), axis=1, keepdims=True) - 1
    extra = jnp.where(lane == 0, extra, 0)
    for part in range(HOT_PARTS):
        chosen = place_row == cold_total + part * share + part_row
        hot_local = jnp.sum(jnp.where(chosen, local_row, 0), axis=1, keepdims=True)
        hot_owner = jnp.sum(jnp.where(chosen, owner_row + 1, 0), axis=1, keepdims=True) - 1
        extra = jnp.where(lane == 1 + part, hot_local, extra)
        extra = jnp.where(lane == 1 + HOT_PARTS + part, hot_owner, extra)
    cold_ref[:, width:] = extra.astype(jnp.float32).astype(jnp.bfloat16)


def pack(request, table, tokens, stored, owners, share):
    count, width = tokens.shape
    return pl.pallas_call(
        functools.partial(pack_kernel, stored, owners, share),
        out_shape=(
            jax.ShapeDtypeStruct((owners * share, width + EXTRA), jnp.bfloat16),
            jax.ShapeDtypeStruct((HOT_PARTS * share, width), jnp.bfloat16),
            jax.ShapeDtypeStruct((count, 1), jnp.int32),
        ),
        in_specs=[whole()] * 3,
        out_specs=(whole(),) * 3,
        compiler_params=params(),
    )(request.reshape(1, -1), table.reshape(1, -1), tokens)


def down_kernel(rank, parts, *refs):
    rows_refs = refs[:parts]
    local_refs = refs[parts : 2 * parts]
    weight_ref = refs[2 * parts]
    out_refs = refs[2 * parts + 1 : 3 * parts + 1]
    totals = refs[3 * parts + 1 :]
    step = pl.program_id(0)
    for rows_ref, total in zip(rows_refs, totals):
        product = lax.dot_general(
            rows_ref[...],
            weight_ref[...],
            (((1,), (1,)), ((), ())),
            preferred_element_type=jnp.float32,
        )

        @pl.when(step == 0)
        def _():
            total[...] = product

        @pl.when(step > 0)
        def _():
            total[...] += product

    @pl.when(step == pl.num_programs(0) - 1)
    def _():
        for local_ref, out_ref, total in zip(local_refs, out_refs, totals):
            local = local_ref[...]
            count = local.shape[0]
            pair = LANES // rank
            lane_block = lax.broadcasted_iota(jnp.int32, (count, LANES), 1) // rank
            summed = jnp.zeros((count, LANES), jnp.float32)
            for j in range(total.shape[1] // LANES):
                hit = lane_block + j * pair == local
                summed = summed + jnp.where(hit, total[:, j * LANES : (j + 1) * LANES], 0.0)
            out = summed[:, :rank]
            for k in range(1, pair):
                out = out + summed[:, k * rank : (k + 1) * rank]
            out_ref[...] = out


def down(row_arrays, locals_, table, rank):
    stored_rank, width = table.shape
    parts = len(row_arrays)
    chunk = 512
    while width % chunk:
        chunk -= LANES
    steps = width // chunk
    return pl.pallas_call(
        functools.partial(down_kernel, rank, parts),
        grid=(steps,),
        out_shape=tuple(jax.ShapeDtypeStruct((r.shape[0], rank), jnp.float32) for r in row_arrays),
        in_specs=[pl.BlockSpec((r.shape[0], chunk), lambda k: (0, k)) for r in row_arrays]
        + [pl.BlockSpec((r.shape[0], 1), lambda k: (0, 0)) for r in row_arrays]
        + [pl.BlockSpec((stored_rank, chunk), lambda k: (0, k))],
        out_specs=tuple(pl.BlockSpec((r.shape[0], rank), lambda k: (0, 0)) for r in row_arrays),
        scratch_shapes=[pltpu.VMEM((r.shape[0], stored_rank), jnp.float32) for r in row_arrays],
        compiler_params=params(),
        cost_estimate=pl.CostEstimate(
            flops=2 * sum(r.shape[0] for r in row_arrays) * stored_rank * width,
            bytes_accessed=2 * stored_rank * width,
            transcendentals=0,
        ),
    )(*row_arrays, *locals_, table)


def up_kernel(rank, own_ref, other_ref, local_ref, weight_ref, out_ref):
    shrunk = (own_ref[...] + other_ref[...]).astype(jnp.bfloat16).astype(jnp.float32)
    count = shrunk.shape[0]
    stored_rank = weight_ref.shape[0]
    pair = LANES // rank
    doubled = jnp.concatenate([shrunk] * pair, axis=1)
    lane_block = lax.broadcasted_iota(jnp.int32, (count, LANES), 1) // rank
    local = local_ref[...]
    spread = jnp.concatenate(
        [
            jnp.where(lane_block + j * pair == local, doubled, 0.0).astype(jnp.bfloat16)
            for j in range(stored_rank // LANES)
        ],
        axis=1,
    )
    out_ref[...] = jnp.dot(spread, weight_ref[...], preferred_element_type=jnp.float32).astype(
        jnp.bfloat16
    )


def up(own, other, local, table):
    count, rank = own.shape
    return pl.pallas_call(
        functools.partial(up_kernel, rank),
        out_shape=jax.ShapeDtypeStruct((count, table.shape[1]), jnp.bfloat16),
        in_specs=[whole()] * 4,
        out_specs=whole(),
        compiler_params=params(),
        cost_estimate=pl.CostEstimate(
            flops=2 * count * table.shape[0] * table.shape[1],
            bytes_accessed=2 * table.shape[0] * table.shape[1],
            transcendentals=0,
        ),
    )(own, other, local, table)


def finish_kernel(
    head, own_ref, other_ref, cold_ref, hot_ref, place_ref, scale_ref, cos_ref, sin_ref, out_ref
):
    count, width = own_ref.shape
    cold_total = cold_ref.shape[0]
    hot_total = hot_ref.shape[0]
    place = place_ref[...]
    from_cold = place == lax.broadcasted_iota(jnp.int32, (count, cold_total), 1)
    from_hot = place - cold_total == lax.broadcasted_iota(jnp.int32, (count, hot_total), 1)
    delta = jnp.dot(
        from_cold.astype(jnp.float32).astype(jnp.bfloat16), cold_ref[...], preferred_element_type=jnp.float32
    ) + jnp.dot(
        from_hot.astype(jnp.float32).astype(jnp.bfloat16), hot_ref[...], preferred_element_type=jnp.float32
    )
    keys = own_ref[...] + other_ref[...] + delta
    cosine = cos_ref[...]
    sine = sin_ref[...]
    for h in range(width // head):
        one = keys[:, h * head : (h + 1) * head]
        normed = (
            one
            * lax.rsqrt(jnp.mean(one * one, axis=-1, keepdims=True) + 1e-06)
            * scale_ref[...]
        )
        turned = pltpu.roll(normed, head // 2, 1)
        out_ref[:, h * head : (h + 1) * head] = (normed * cosine + turned * sine).astype(jnp.bfloat16)


def finish(own, other, cold, hot, place, scale, cosine, sine):
    return pl.pallas_call(
        functools.partial(finish_kernel, scale.shape[0]),
        out_shape=jax.ShapeDtypeStruct(own.shape, jnp.bfloat16),
        in_specs=[whole()] * 8,
        out_specs=whole(),
        compiler_params=params(),
    )(own, other, cold, hot, place, scale.reshape(1, -1), cosine, sine)


def rope_tables(head, cached_token_length):
    half = head // 2
    inv_freq = rope_theta ** (-(jnp.arange(half, dtype=jnp.float32) * 2.0) / head)
    angles = cached_token_length.astype(jnp.float32)[:, None] * inv_freq[None, :]
    cosine = jnp.cos(angles)
    sine = jnp.sin(angles)
    return jnp.concatenate([cosine, cosine], axis=1), jnp.concatenate([-sine, sine], axis=1)


def swap(x):
    return lax.ppermute(x, "tensor", [(0, 1), (1, 0)])


def on_device(
    tokens,
    base_key_matrix,
    adapter_down_weight,
    adapter_up_weight,
    key_norm_scale,
    request_adapter,
    adapter_slot_table,
    cached_token_length,
):
    row_count, half_width = tokens.shape
    stored, rank, _ = adapter_down_weight.shape
    owners = lax.axis_size("dp")
    me = lax.axis_index("dp")
    side = lax.axis_index("tensor")
    share = (row_count + owners + 2) // (owners + 3)
    hot_count = HOT_PARTS * share
    down_table = adapter_down_weight.reshape(stored * rank, half_width)
    up_table = adapter_up_weight.reshape(stored * rank, -1)
    features = up_table.shape[1]

    cold_send, hot_send, place = pack(
        request_adapter, adapter_slot_table, tokens, stored, owners, share
    )

    ring = ring_order(owners)
    to_next = [(ring[i], ring[(i + 1) % owners]) for i in range(owners)]
    to_last = [(b, a) for a, b in to_next]
    spots = [0] * owners
    for spot, index in enumerate(ring):
        spots[index] = spot
    my_spot = jnp.take(jnp.array(spots, jnp.int32), me)
    ring_array = jnp.array(ring, jnp.int32)

    def source(distance):
        return jnp.take(ring_array, (my_spot + distance) % owners)

    cut = hot_count // 2 // 8 * 8 if hot_count >= 16 else hot_count // 2
    forward = backward = hot_send
    arrivals = [(0, hot_send)]
    for step in range(1, owners // 2):
        forward = lax.ppermute(forward, "dp", to_next)
        backward = lax.ppermute(backward, "dp", to_last)
        arrivals += [(-step, forward), (step, backward)]
    last_front = lax.ppermute(forward[:cut], "dp", to_next)
    last_rear = lax.ppermute(backward[cut:], "dp", to_last)

    got = lax.all_to_all(
        cold_send.reshape(owners, share, half_width + EXTRA), "dp", split_axis=0, concat_axis=0, tiled=True
    )
    routing = got[:, :, half_width : half_width + 1 + 2 * HOT_PARTS].astype(jnp.int32)
    cold_local = routing[:, :, 0].reshape(owners * share, 1)
    hot_local = jnp.where(
        routing[:, :, 1 + HOT_PARTS : 1 + 2 * HOT_PARTS] == me, routing[:, :, 1 : 1 + HOT_PARTS], -1
    )
    hot_local = jnp.transpose(hot_local, (0, 2, 1)).reshape(owners, hot_count)
    order = jnp.stack([source(d) for d, _ in arrivals] + [source(owners // 2)])
    hot_local = jnp.take(hot_local, order, axis=0)

    base = jnp.dot(tokens, base_key_matrix, preferred_element_type=jnp.float32)
    base_own = lax.dynamic_slice_in_dim(base, side * features, features, 1)
    base_other = swap(lax.dynamic_slice_in_dim(base, (1 - side) * features, features, 1))

    got_rows = got.reshape(owners * share, half_width + EXTRA)[:, :half_width]
    (cold_part,) = down([got_rows], [cold_local], down_table, rank)
    cold_delta = up(cold_part, swap(cold_part), cold_local, up_table)
    cold_back = lax.all_to_all(
        cold_delta.reshape(owners, share, features), "dp", split_axis=0, concat_axis=0, tiled=True
    ).reshape(owners * share, features)

    groups = [[0]] + [[2 * s - 1, 2 * s] for s in range(1, owners // 2)]
    columns = [hot_local[i].reshape(hot_count, 1) for i in range(owners)]
    parts = []
    for group in groups:
        parts += down([arrivals[i][1] for i in group], [columns[i] for i in group], down_table, rank)
    parts += down(
        [last_front, last_rear], [columns[-1][:cut], columns[-1][cut:]], down_table, rank
    )
    hot_part = jnp.concatenate(parts, axis=0)
    hot_delta = up(hot_part, swap(hot_part), hot_local.reshape(-1, 1), up_table)
    by_source = jnp.zeros((owners,), jnp.int32).at[order].set(jnp.arange(owners, dtype=jnp.int32))
    hot_return = jnp.take(hot_delta.reshape(owners, hot_count, features), by_source, axis=0)
    hot_got = lax.all_to_all(hot_return, "dp", split_axis=0, concat_axis=0, tiled=True)
    hot_back = jnp.sum(hot_got.astype(jnp.float32), axis=0).astype(jnp.bfloat16)

    cosine, sine = rope_tables(key_norm_scale.shape[0], cached_token_length)
    return finish(base_own, base_other, cold_back, hot_back, place, key_norm_scale, cosine, sine)


def solution(mesh):
    placed = (
        P(("groups", "dp"), "tensor"),
        P("tensor", None),
        P(("groups", "dp"), None, "tensor"),
        P(("groups", "dp"), None, "tensor"),
        P(),
        P(("groups", "dp")),
        P("groups"),
        P(("groups", "dp")),
    )
    return jax.shard_map(
        on_device,
        mesh=mesh,
        in_specs=placed,
        out_specs=P(("groups", "dp"), "tensor"),
        check_vma=False,
    )
```

```python
import functools

import jax
import jax.numpy as jnp
from jax import lax
from jax.experimental import pallas as pl
from jax.experimental.pallas import tpu as pltpu
from jax.sharding import PartitionSpec as P

rope_theta = 1000000.0
LANES = 128
EXTRA = 128
HOT_PARTS = 3
VMEM_BYTES = 60 * 1024 * 1024


def whole():
    return pl.BlockSpec(memory_space=pltpu.VMEM)


def params():
    return pltpu.CompilerParams(vmem_limit_bytes=VMEM_BYTES)


def ring_order(owners):
    return [i for i in range(0, owners, 2)] + [i for i in range(owners - 1, 0, -2)]


def to_column(row):
    count = row.shape[1]
    square = lax.broadcasted_iota(jnp.int32, (count, count), 0) == lax.broadcasted_iota(
        jnp.int32, (count, count), 1
    )
    return jnp.sum(jnp.where(square, row, 0), axis=1, keepdims=True)


def pack_kernel(
    stored, owners, share, request_ref, table_ref, tokens_ref, cold_ref, hot_ref, place_ref, busy_ref
):
    count = request_ref.shape[1]
    width = tokens_ref.shape[1]
    request_col = to_column(request_ref[...])
    adapters = table_ref.shape[1]
    match = request_col == lax.broadcasted_iota(jnp.int32, (count, adapters), 1)
    slot_col = jnp.sum(jnp.where(match, table_ref[...], 0), axis=1, keepdims=True)
    row_id = lax.broadcasted_iota(jnp.int32, (count, count), 0)
    col_id = lax.broadcasted_iota(jnp.int32, (count, count), 1)
    slot_row = jnp.sum(jnp.where(row_id == col_id, slot_col, 0), axis=0, keepdims=True)
    owner_col = slot_col // stored
    owner_row = slot_row // stored
    same = owner_col == owner_row
    rank_col = jnp.sum(jnp.where(same & (col_id < row_id), 1, 0), axis=1, keepdims=True)
    rank_row = jnp.sum(jnp.where(same & (row_id < col_id), 1, 0), axis=0, keepdims=True)
    cold_total = owners * share
    hot_total = HOT_PARTS * share

    def place(owner, rank):
        return jnp.where(rank < share, owner * share + rank, cold_total + rank - share)

    place_ref[...] = place(owner_col, rank_col)
    busy_ref[...] = jnp.max(jnp.where(rank_row >= share, owner_row, 0), axis=1, keepdims=True)
    place_row = place(owner_row, rank_row)
    local_row = slot_row - owner_row * stored
    tokens = tokens_ref[...]
    for first, total, out_ref in ((0, cold_total, cold_ref), (cold_total, hot_total, hot_ref)):
        pick = place_row - first == lax.broadcasted_iota(jnp.int32, (total, count), 0)
        out_ref[:, :width] = jnp.dot(
            pick.astype(jnp.float32).astype(jnp.bfloat16), tokens, preferred_element_type=jnp.float32
        ).astype(jnp.bfloat16)
        owner = jnp.sum(jnp.where(pick, owner_row + 1, 0), axis=1, keepdims=True) - 1
        local = jnp.sum(jnp.where(pick, local_row, 0), axis=1, keepdims=True)
        lane = lax.broadcasted_iota(jnp.int32, (total, EXTRA), 1)
        extra = jnp.where(lane == 0, owner, jnp.where(lane == 1, local, 0))
        out_ref[:, width:] = extra.astype(jnp.float32).astype(jnp.bfloat16)


def pack(request, table, tokens, stored, owners, share):
    count, width = tokens.shape
    return pl.pallas_call(
        functools.partial(pack_kernel, stored, owners, share),
        out_shape=(
            jax.ShapeDtypeStruct((owners * share, width + EXTRA), jnp.bfloat16),
            jax.ShapeDtypeStruct((HOT_PARTS * share, width + EXTRA), jnp.bfloat16),
            jax.ShapeDtypeStruct((count, 1), jnp.int32),
            jax.ShapeDtypeStruct((1, 1), jnp.int32),
        ),
        in_specs=[whole()] * 3,
        out_specs=(whole(),) * 4,
        compiler_params=params(),
    )(request.reshape(1, -1), table.reshape(1, -1), tokens)


def local_column(extra, me):
    extra = extra.astype(jnp.float32)
    return jnp.where(extra[:, 0:1] == me.astype(jnp.float32), extra[:, 1:2], -1.0).astype(jnp.int32)


def down_kernel(rank, parts, me_ref, *refs):
    rows_refs = refs[:parts]
    extra_refs = refs[parts : 2 * parts]
    weight_ref, out_ref, total = refs[2 * parts :]
    step = pl.program_id(0)
    rows = rows_refs[0][...] if parts == 1 else jnp.concatenate([r[...] for r in rows_refs], axis=0)
    product = lax.dot_general(
        rows, weight_ref[...], (((1,), (1,)), ((), ())), preferred_element_type=jnp.float32
    )

    @pl.when(step == 0)
    def _():
        total[...] = product

    @pl.when(step > 0)
    def _():
        total[...] += product

    @pl.when(step == pl.num_programs(0) - 1)
    def _():
        local = jnp.concatenate([local_column(r[...], me_ref[0]) for r in extra_refs], axis=0)
        count = local.shape[0]
        pair = LANES // rank
        lane_block = lax.broadcasted_iota(jnp.int32, (count, LANES), 1) // rank
        summed = jnp.zeros((count, LANES), jnp.float32)
        for j in range(total.shape[1] // LANES):
            hit = lane_block + j * pair == local
            summed = summed + jnp.where(hit, total[:, j * LANES : (j + 1) * LANES], 0.0)
        out = summed[:, :rank]
        for k in range(1, pair):
            out = out + summed[:, k * rank : (k + 1) * rank]
        out_ref[...] = out


def down(me, row_arrays, table, rank):
    stored_rank, width = table.shape
    parts = len(row_arrays)
    count = sum(r.shape[0] for r in row_arrays)
    chunk = 512
    while width % chunk:
        chunk -= LANES
    last = width // EXTRA
    return pl.pallas_call(
        functools.partial(down_kernel, rank, parts),
        grid_spec=pltpu.PrefetchScalarGridSpec(
            num_scalar_prefetch=1,
            grid=(width // chunk,),
            in_specs=[pl.BlockSpec((r.shape[0], chunk), lambda k, m: (0, k)) for r in row_arrays]
            + [pl.BlockSpec((r.shape[0], EXTRA), lambda k, m: (0, last)) for r in row_arrays]
            + [pl.BlockSpec((stored_rank, chunk), lambda k, m: (0, k))],
            out_specs=pl.BlockSpec((count, rank), lambda k, m: (0, 0)),
            scratch_shapes=[pltpu.VMEM((count, stored_rank), jnp.float32)],
        ),
        out_shape=jax.ShapeDtypeStruct((count, rank), jnp.float32),
        compiler_params=params(),
        cost_estimate=pl.CostEstimate(
            flops=2 * count * stored_rank * width,
            bytes_accessed=2 * stored_rank * width,
            transcendentals=0,
        ),
    )(me, *row_arrays, *row_arrays, table)


def spread_product(shrunk, local, weight, rank):
    count = shrunk.shape[0]
    pair = LANES // rank
    doubled = jnp.concatenate([shrunk] * pair, axis=1)
    lane_block = lax.broadcasted_iota(jnp.int32, (count, LANES), 1) // rank
    spread = jnp.concatenate(
        [
            jnp.where(lane_block + j * pair == local, doubled, 0.0).astype(jnp.bfloat16)
            for j in range(weight.shape[0] // LANES)
        ],
        axis=1,
    )
    return jnp.dot(spread, weight, preferred_element_type=jnp.float32).astype(jnp.bfloat16)


def up_kernel(rank, blocks, me_ref, to_ref, *refs):
    own_refs = refs[:blocks]
    other_refs = refs[blocks : 2 * blocks]
    count_extra = len(refs) - 2 * blocks - 2
    extra_refs = refs[2 * blocks : 2 * blocks + count_extra]
    weight_ref = refs[-2]
    out_ref = refs[-1]
    own = jnp.concatenate([r[...] for r in own_refs], axis=0)
    other = jnp.concatenate([r[...] for r in other_refs], axis=0)
    local = jnp.concatenate([local_column(r[...], me_ref[0]) for r in extra_refs], axis=0)
    shrunk = (own + other).astype(jnp.bfloat16).astype(jnp.float32)
    out_ref[...] = spread_product(shrunk, local, weight_ref[...], rank)


def up_cold(me, own, other, rows, table):
    count, rank = own.shape
    last = (rows.shape[1] - EXTRA) // EXTRA
    return pl.pallas_call(
        functools.partial(up_kernel, rank, 1),
        grid_spec=pltpu.PrefetchScalarGridSpec(
            num_scalar_prefetch=2,
            grid=(1,),
            in_specs=[
                pl.BlockSpec((count, rank), lambda i, m, t: (0, 0)),
                pl.BlockSpec((count, rank), lambda i, m, t: (0, 0)),
                pl.BlockSpec((count, EXTRA), lambda i, m, t: (0, last)),
                pl.BlockSpec(table.shape, lambda i, m, t: (0, 0)),
            ],
            out_specs=pl.BlockSpec((count, table.shape[1]), lambda i, m, t: (0, 0)),
        ),
        out_shape=jax.ShapeDtypeStruct((count, table.shape[1]), jnp.bfloat16),
        compiler_params=params(),
        cost_estimate=pl.CostEstimate(
            flops=2 * count * table.shape[0] * table.shape[1],
            bytes_accessed=2 * table.shape[0] * table.shape[1],
            transcendentals=0,
        ),
    )(me, me, own, other, rows, table)


def up_hot_kernel(rank, sizes, extra_counts, keeps, me_ref, to_ref, *refs):
    groups = len(sizes)
    own_refs = refs[:groups]
    other_refs = refs[groups : 2 * groups]
    extra_refs = refs[2 * groups : 2 * groups + sum(extra_counts)]
    weight_ref, out_ref, buffer, sems = refs[-4:]
    local, at = [], 0
    for n in extra_counts:
        local += [local_column(r[...], me_ref[0]) for r in extra_refs[at : at + n]]
        at += n
    local = jnp.concatenate(local, axis=0)
    own = jnp.concatenate([r[...] for r in own_refs], axis=0)
    other = jnp.concatenate([r[...] for r in other_refs], axis=0)
    shrunk = (own + other).astype(jnp.bfloat16).astype(jnp.float32)
    product = spread_product(shrunk, local, weight_ref[...], rank).astype(jnp.float32)
    blocks, count = buffer.shape[:2]
    copies = []
    for b in range(blocks):
        buffer[b] = product[b * count : (b + 1) * count].astype(jnp.bfloat16)
        copies.append(pltpu.make_async_copy(buffer.at[b], out_ref.at[to_ref[b]], sems.at[b]))
        copies[-1].start()
    for copy in copies:
        copy.wait()


def up_hot(me, targets, owns, others, row_groups, table, count, owners, earlier=None):
    rank = owns[0].shape[1]
    blocks = targets.shape[0]
    arrays = [r for group in row_groups for r in group]
    last = (arrays[0].shape[1] - EXTRA) // EXTRA
    full = [pl.BlockSpec(x.shape, lambda i, m, t: (0, 0)) for x in owns]
    kept = [] if earlier is None else [earlier]
    return pl.pallas_call(
        functools.partial(
            up_hot_kernel, rank, [x.shape[0] for x in owns], [len(g) for g in row_groups], len(kept)
        ),
        grid_spec=pltpu.PrefetchScalarGridSpec(
            num_scalar_prefetch=2,
            grid=(1,),
            in_specs=full
            + full
            + [pl.BlockSpec((r.shape[0], EXTRA), lambda i, m, t: (0, last)) for r in arrays]
            + [pl.BlockSpec(memory_space=pl.ANY) for _ in kept]
            + [pl.BlockSpec(table.shape, lambda i, m, t: (0, 0))],
            out_specs=pl.BlockSpec(memory_space=pl.ANY),
            scratch_shapes=[
                pltpu.VMEM((blocks, count, table.shape[1]), jnp.bfloat16),
                pltpu.SemaphoreType.DMA((blocks,)),
            ],
        ),
        out_shape=jax.ShapeDtypeStruct((owners, count, table.shape[1]), jnp.bfloat16),
        input_output_aliases={2 + 2 * len(owns) + len(arrays): 0} if kept else {},
        compiler_params=params(),
        cost_estimate=pl.CostEstimate(
            flops=2 * blocks * count * table.shape[0] * table.shape[1],
            bytes_accessed=2 * table.shape[0] * table.shape[1],
            transcendentals=0,
        ),
    )(me, targets, *owns, *others, *arrays, *kept, table)


def finish_kernel(
    head, busy_ref, own_ref, other_ref, cold_ref, hot_ref, place_ref, scale_ref, cos_ref, sin_ref, out_ref
):
    count, width = own_ref.shape
    cold_total = cold_ref.shape[0]
    hot_total = hot_ref.shape[1]
    place = place_ref[...]
    from_cold = place == lax.broadcasted_iota(jnp.int32, (count, cold_total), 1)
    from_hot = place - cold_total == lax.broadcasted_iota(jnp.int32, (count, hot_total), 1)
    delta = jnp.dot(
        from_cold.astype(jnp.float32).astype(jnp.bfloat16), cold_ref[...], preferred_element_type=jnp.float32
    ) + jnp.dot(
        from_hot.astype(jnp.float32).astype(jnp.bfloat16), hot_ref[0], preferred_element_type=jnp.float32
    )
    keys = own_ref[...] + other_ref[...] + delta
    cosine = cos_ref[...]
    sine = sin_ref[...]
    for h in range(width // head):
        one = keys[:, h * head : (h + 1) * head]
        normed = (
            one
            * lax.rsqrt(jnp.mean(one * one, axis=-1, keepdims=True) + 1e-06)
            * scale_ref[...]
        )
        turned = pltpu.roll(normed, head // 2, 1)
        out_ref[:, h * head : (h + 1) * head] = (normed * cosine + turned * sine).astype(jnp.bfloat16)


def finish(busy, own, other, cold, hot, place, scale, cosine, sine):
    def full(x):
        return pl.BlockSpec(x.shape, lambda i, b: (0, 0))

    scale = scale.reshape(1, -1)
    return pl.pallas_call(
        functools.partial(finish_kernel, scale.shape[1]),
        grid_spec=pltpu.PrefetchScalarGridSpec(
            num_scalar_prefetch=1,
            grid=(1,),
            in_specs=[
                full(own),
                full(other),
                full(cold),
                pl.BlockSpec((1,) + hot.shape[1:], lambda i, b: (b[0], 0, 0)),
                full(place),
                full(scale),
                full(cosine),
                full(sine),
            ],
            out_specs=full(own),
        ),
        out_shape=jax.ShapeDtypeStruct(own.shape, jnp.bfloat16),
        compiler_params=params(),
    )(busy, own, other, cold, hot, place, scale, cosine, sine)


def after(value, *earlier):
    return lax.optimization_barrier((value,) + earlier)[0]


def rope_tables(head, cached_token_length):
    half = head // 2
    inv_freq = rope_theta ** (-(jnp.arange(half, dtype=jnp.float32) * 2.0) / head)
    angles = cached_token_length.astype(jnp.float32)[:, None] * inv_freq[None, :]
    cosine = jnp.cos(angles)
    sine = jnp.sin(angles)
    return jnp.concatenate([cosine, cosine], axis=1), jnp.concatenate([-sine, sine], axis=1)


def swap(x):
    return lax.ppermute(x, "tensor", [(0, 1), (1, 0)])


def on_device(
    tokens,
    base_key_matrix,
    adapter_down_weight,
    adapter_up_weight,
    key_norm_scale,
    request_adapter,
    adapter_slot_table,
    cached_token_length,
):
    row_count, half_width = tokens.shape
    stored, rank, _ = adapter_down_weight.shape
    owners = lax.axis_size("dp")
    me = lax.axis_index("dp")
    side = lax.axis_index("tensor")
    share = (row_count + owners + 2) // (owners + 3)
    hot_count = HOT_PARTS * share
    down_table = adapter_down_weight.reshape(stored * rank, half_width)
    up_table = adapter_up_weight.reshape(stored * rank, -1)
    features = up_table.shape[1]

    cold_send, hot_send, place, busy = pack(
        request_adapter, adapter_slot_table, tokens, stored, owners, share
    )
    here = me.reshape(1).astype(jnp.int32)

    ring = ring_order(owners)
    to_next = [(ring[i], ring[(i + 1) % owners]) for i in range(owners)]
    to_last = [(b, a) for a, b in to_next]
    distances = [0] + [d for s in range(1, owners // 2) for d in (-s, s)] + [owners // 2]
    sources = [[0] * owners for _ in ring]
    for spot, index in enumerate(ring):
        sources[index] = [ring[(spot + d) % owners] for d in distances]
    order = lax.dynamic_index_in_dim(jnp.array(sources, jnp.int32), me, 0, keepdims=False)

    cut = hot_count // 2 // 8 * 8 if hot_count >= 16 else hot_count // 2
    half_way = owners // 2
    forward = lax.ppermute(hot_send, "dp", to_next)
    backward = lax.ppermute(hot_send, "dp", to_last)
    got = lax.all_to_all(
        cold_send.reshape(owners, share, half_width + EXTRA), "dp", split_axis=0, concat_axis=0, tiled=True
    ).reshape(owners * share, half_width + EXTRA)

    base = jnp.dot(tokens, base_key_matrix, preferred_element_type=jnp.float32)
    base_own = lax.dynamic_slice_in_dim(base, side * features, features, 1)
    base_other = swap(lax.dynamic_slice_in_dim(base, (1 - side) * features, features, 1))
    cosine, sine = rope_tables(key_norm_scale.shape[0], cached_token_length)

    row_groups = [[hot_send]]
    part = down(here, [hot_send], down_table, rank)
    parts, others = [part], [swap(part)]
    todo = [part, base]
    for step in range(1, half_way):
        forward, backward, *_ = lax.optimization_barrier((forward, backward, *todo))
        group = [forward, backward]
        if step < half_way - 1:
            forward = lax.ppermute(forward, "dp", to_next)
            backward = lax.ppermute(backward, "dp", to_last)
        else:
            last_front = lax.ppermute(forward[:cut], "dp", to_next)
            last_rear = lax.ppermute(backward[cut:], "dp", to_last)
        row_groups.append(group)
        part = down(here, group, down_table, rank)
        parts.append(part)
        others.append(swap(part))
        todo = [part]
        if step == max(half_way - 2, 1):
            cold_part = down(here, [got], down_table, rank)
            cold_delta = up_cold(here, cold_part, swap(cold_part), got, up_table)
            cold_back = lax.all_to_all(
                cold_delta.reshape(owners, share, features), "dp", split_axis=0, concat_axis=0, tiled=True
            ).reshape(owners * share, features)
            todo += [cold_delta]

    hot_delta = up_hot(
        here, order[: owners - 1], parts, others, row_groups, up_table, hot_count, owners
    )
    last_front, last_rear, hot_delta, cold_back = lax.optimization_barrier(
        (last_front, last_rear, hot_delta, cold_back)
    )
    group = [last_front, last_rear]
    part = down(here, group, down_table, rank)
    hot_delta = up_hot(
        here,
        order[owners - 1 :],
        [part],
        [swap(part)],
        [group],
        up_table,
        hot_count,
        owners,
        hot_delta,
    )
    hot_back = lax.all_to_all(hot_delta, "dp", split_axis=0, concat_axis=0, tiled=True)
    return finish(
        busy.reshape(1), base_own, base_other, cold_back, hot_back, place, key_norm_scale, cosine, sine
    )


def solution(mesh):
    placed = (
        P(("groups", "dp"), "tensor"),
        P("tensor", None),
        P(("groups", "dp"), None, "tensor"),
        P(("groups", "dp"), None, "tensor"),
        P(),
        P(("groups", "dp")),
        P("groups"),
        P(("groups", "dp")),
    )
    return jax.shard_map(
        on_device,
        mesh=mesh,
        in_specs=placed,
        out_specs=P(("groups", "dp"), "tensor"),
        check_vma=False,
    )
```

```python
import functools

import jax
import jax.numpy as jnp
from jax import lax
from jax.experimental import pallas as pl
from jax.experimental.pallas import tpu as pltpu
from jax.sharding import PartitionSpec as P

rope_theta = 1000000.0
LANES = 128
EXTRA = 128
HOT_PARTS = 3
ALL_VMEM = 60 * 1024 * 1024
SOME_VMEM = 16 * 1024 * 1024


def whole():
    return pl.BlockSpec(memory_space=pltpu.VMEM)


def scalars():
    return pl.BlockSpec(memory_space=pltpu.SMEM)


def params(limit=SOME_VMEM):
    return pltpu.CompilerParams(vmem_limit_bytes=limit)


def ring_order(owners):
    return [i for i in range(0, owners, 2)] + [i for i in range(owners - 1, 0, -2)]


def to_column(row):
    count = row.shape[1]
    square = lax.broadcasted_iota(jnp.int32, (count, count), 0) == lax.broadcasted_iota(
        jnp.int32, (count, count), 1
    )
    return jnp.sum(jnp.where(square, row, 0), axis=1, keepdims=True)


def pack_kernel(
    stored, owners, share, pieces, request_ref, table_ref, tokens_ref, cold_ref, *refs
):
    hot_refs, (place_ref, busy_ref) = refs[: len(pieces)], refs[len(pieces) :]
    count = request_ref.shape[1]
    width = tokens_ref.shape[1]
    request_col = to_column(request_ref[...])
    adapters = table_ref.shape[1]
    match = request_col == lax.broadcasted_iota(jnp.int32, (count, adapters), 1)
    slot_col = jnp.sum(jnp.where(match, table_ref[...], 0), axis=1, keepdims=True)
    row_id = lax.broadcasted_iota(jnp.int32, (count, count), 0)
    col_id = lax.broadcasted_iota(jnp.int32, (count, count), 1)
    slot_row = jnp.sum(jnp.where(row_id == col_id, slot_col, 0), axis=0, keepdims=True)
    owner_col = slot_col // stored
    owner_row = slot_row // stored
    same = owner_col == owner_row
    rank_col = jnp.sum(jnp.where(same & (col_id < row_id), 1, 0), axis=1, keepdims=True)
    rank_row = jnp.sum(jnp.where(same & (row_id < col_id), 1, 0), axis=0, keepdims=True)
    cold_total = owners * share

    def place(owner, rank):
        return jnp.where(rank < share, owner * share + rank, cold_total + rank - share)

    place_ref[...] = place(owner_col, rank_col)
    busy_ref[...] = jnp.max(jnp.where(rank_row >= share, owner_row, 0), axis=1, keepdims=True)
    place_row = place(owner_row, rank_row)
    local_row = slot_row - owner_row * stored
    tokens = tokens_ref[...]
    outs, first = [(0, cold_total, cold_ref)], cold_total
    for total, out_ref in zip(pieces, hot_refs):
        outs.append((first, total, out_ref))
        first += total
    for first, total, out_ref in outs:
        pick = place_row - first == lax.broadcasted_iota(jnp.int32, (total, count), 0)
        out_ref[:, :width] = jnp.dot(
            pick.astype(jnp.float32).astype(jnp.bfloat16), tokens, preferred_element_type=jnp.float32
        ).astype(jnp.bfloat16)
        owner = jnp.sum(jnp.where(pick, owner_row + 1, 0), axis=1, keepdims=True) - 1
        local = jnp.sum(jnp.where(pick, local_row, 0), axis=1, keepdims=True)
        lane = lax.broadcasted_iota(jnp.int32, (total, EXTRA), 1)
        extra = jnp.where(lane == 0, owner, jnp.where(lane == 1, local, 0))
        out_ref[:, width:] = extra.astype(jnp.float32).astype(jnp.bfloat16)


def pack(request, table, tokens, stored, owners, share, pieces):
    count, width = tokens.shape
    return pl.pallas_call(
        functools.partial(pack_kernel, stored, owners, share, pieces),
        out_shape=(
            jax.ShapeDtypeStruct((owners * share, width + EXTRA), jnp.bfloat16),
            *(jax.ShapeDtypeStruct((n, width + EXTRA), jnp.bfloat16) for n in pieces),
            jax.ShapeDtypeStruct((count, 1), jnp.int32),
            jax.ShapeDtypeStruct((1, 1), jnp.int32),
        ),
        in_specs=[whole()] * 3,
        out_specs=(whole(),) * (3 + len(pieces)),
        compiler_params=params(ALL_VMEM),
    )(request.reshape(1, -1), table.reshape(1, -1), tokens)


def down_kernel(rank, parts, me_ref, *refs):
    rows_refs = refs[:parts]
    weight_ref, out_ref, local_ref = refs[parts:]
    width = weight_ref.shape[1]
    extra = jnp.concatenate([r[:, width:].astype(jnp.float32) for r in rows_refs], axis=0).T
    local = jnp.where(extra[0:1] == me_ref[0].astype(jnp.float32), extra[1:2], -1.0)
    rows = jnp.concatenate([r[:, :width] for r in rows_refs], axis=0)
    block = 4 * rank
    out = jnp.zeros(out_ref.shape, jnp.float32)
    for first in range(0, weight_ref.shape[0], block):
        product = lax.dot_general(
            weight_ref[first : first + block, :],
            rows,
            (((1,), (1,)), ((), ())),
            preferred_element_type=jnp.float32,
        )
        for j in range(block // rank):
            mine = local == float(first // rank + j)
            out = out + jnp.where(mine, product[j * rank : (j + 1) * rank, :], 0.0)
    out_ref[...] = out
    local_ref[...] = local


def down(me, row_arrays, table, rank):
    stored_rank, width = table.shape
    count = sum(r.shape[0] for r in row_arrays)
    return pl.pallas_call(
        functools.partial(down_kernel, rank, len(row_arrays)),
        in_specs=[scalars()] + [whole()] * (len(row_arrays) + 1),
        out_specs=(whole(), whole()),
        out_shape=(
            jax.ShapeDtypeStruct((rank, count), jnp.float32),
            jax.ShapeDtypeStruct((1, count), jnp.float32),
        ),
        compiler_params=params(),
        cost_estimate=pl.CostEstimate(
            flops=2 * count * stored_rank * width,
            bytes_accessed=2 * stored_rank * width,
            transcendentals=0,
        ),
    )(me, *row_arrays, table)


def update(own_ref, other_ref, local_ref, weight_ref):
    rank, count = own_ref.shape
    pair = LANES // rank
    shrunk = (own_ref[...] + other_ref[...]).astype(jnp.bfloat16).astype(jnp.float32)
    doubled = jnp.concatenate([shrunk] * pair, axis=0).T
    local = jnp.broadcast_to(local_ref[...], (LANES, count)).T.astype(jnp.int32)
    lane_block = lax.broadcasted_iota(jnp.int32, (count, LANES), 1) // rank
    spread = jnp.concatenate(
        [
            jnp.where(lane_block + j * pair == local, doubled, 0.0).astype(jnp.bfloat16)
            for j in range(weight_ref.shape[0] // LANES)
        ],
        axis=1,
    )
    return jnp.dot(spread, weight_ref[...], preferred_element_type=jnp.float32)


def up_cold_kernel(own_ref, other_ref, local_ref, weight_ref, out_ref):
    out_ref[...] = update(own_ref, other_ref, local_ref, weight_ref).astype(jnp.bfloat16)


def up_cost(count, table):
    return pl.CostEstimate(
        flops=2 * count * table.shape[0] * table.shape[1],
        bytes_accessed=2 * table.shape[0] * table.shape[1],
        transcendentals=0,
    )


def up_cold(own, other, local, table):
    count = own.shape[1]
    return pl.pallas_call(
        up_cold_kernel,
        in_specs=[whole()] * 4,
        out_specs=whole(),
        out_shape=jax.ShapeDtypeStruct((count, table.shape[1]), jnp.bfloat16),
        compiler_params=params(),
        cost_estimate=up_cost(count, table),
    )(own, other, local, table)


def up_hot_kernel(blocks, to_ref, own_ref, other_ref, local_ref, weight_ref, *refs):
    out_ref, buffer, sems = refs[-3:]
    product = update(own_ref, other_ref, local_ref, weight_ref)
    count = buffer.shape[1]
    copies = []
    for b in range(blocks):
        buffer[b] = product[b * count : (b + 1) * count].astype(jnp.bfloat16)
        copies.append(pltpu.make_async_copy(buffer.at[b], out_ref.at[to_ref[b]], sems.at[b]))
        copies[-1].start()
    for copy in copies:
        copy.wait()


def up_hot(targets, own, other, local, table, owners, earlier):
    blocks = targets.shape[0]
    count = own.shape[1] // blocks
    kept = [] if earlier is None else [earlier]
    return pl.pallas_call(
        functools.partial(up_hot_kernel, blocks),
        in_specs=[scalars()] + [whole()] * 4 + [pl.BlockSpec(memory_space=pl.ANY) for _ in kept],
        out_specs=pl.BlockSpec(memory_space=pl.ANY),
        scratch_shapes=[
            pltpu.VMEM((blocks, count, table.shape[1]), jnp.bfloat16),
            pltpu.SemaphoreType.DMA((blocks,)),
        ],
        out_shape=jax.ShapeDtypeStruct((owners, count, table.shape[1]), jnp.bfloat16),
        input_output_aliases={5: 0} if kept else {},
        compiler_params=params(),
        cost_estimate=up_cost(blocks * count, table),
    )(targets, own, other, local, table, *kept)


def finish_kernel(
    head, busy_ref, own_ref, other_ref, cold_ref, hot_ref, place_ref, scale_ref, cos_ref, sin_ref, out_ref
):
    count, width = own_ref.shape
    cold_total = cold_ref.shape[0]
    hot_total = hot_ref.shape[1]
    place = place_ref[...]
    from_cold = place == lax.broadcasted_iota(jnp.int32, (count, cold_total), 1)
    from_hot = place - cold_total == lax.broadcasted_iota(jnp.int32, (count, hot_total), 1)
    delta = jnp.dot(
        from_cold.astype(jnp.float32).astype(jnp.bfloat16), cold_ref[...], preferred_element_type=jnp.float32
    ) + jnp.dot(
        from_hot.astype(jnp.float32).astype(jnp.bfloat16), hot_ref[0], preferred_element_type=jnp.float32
    )
    keys = own_ref[...] + other_ref[...] + delta
    cosine = cos_ref[...]
    sine = sin_ref[...]
    for h in range(width // head):
        one = keys[:, h * head : (h + 1) * head]
        normed = (
            one
            * lax.rsqrt(jnp.mean(one * one, axis=-1, keepdims=True) + 1e-06)
            * scale_ref[...]
        )
        turned = pltpu.roll(normed, head // 2, 1)
        out_ref[:, h * head : (h + 1) * head] = (normed * cosine + turned * sine).astype(jnp.bfloat16)


def finish(busy, own, other, cold, hot, place, scale, cosine, sine):
    def full(x):
        return pl.BlockSpec(x.shape, lambda i, b: (0, 0))

    scale = scale.reshape(1, -1)
    return pl.pallas_call(
        functools.partial(finish_kernel, scale.shape[1]),
        grid_spec=pltpu.PrefetchScalarGridSpec(
            num_scalar_prefetch=1,
            grid=(1,),
            in_specs=[
                full(own),
                full(other),
                full(cold),
                pl.BlockSpec((1,) + hot.shape[1:], lambda i, b: (b[0], 0, 0)),
                full(place),
                full(scale),
                full(cosine),
                full(sine),
            ],
            out_specs=full(own),
        ),
        out_shape=jax.ShapeDtypeStruct(own.shape, jnp.bfloat16),
        compiler_params=params(),
    )(busy, own, other, cold, hot, place, scale, cosine, sine)


def after(value, *earlier):
    return lax.optimization_barrier((value,) + earlier)[0]


def rope_tables(head, cached_token_length):
    half = head // 2
    inv_freq = rope_theta ** (-(jnp.arange(half, dtype=jnp.float32) * 2.0) / head)
    angles = cached_token_length.astype(jnp.float32)[:, None] * inv_freq[None, :]
    cosine = jnp.cos(angles)
    sine = jnp.sin(angles)
    return jnp.concatenate([cosine, cosine], axis=1), jnp.concatenate([-sine, sine], axis=1)


def swap(x):
    return lax.ppermute(x, "tensor", [(0, 1), (1, 0)])


def on_device(
    tokens,
    base_key_matrix,
    adapter_down_weight,
    adapter_up_weight,
    key_norm_scale,
    request_adapter,
    adapter_slot_table,
    cached_token_length,
):
    row_count, half_width = tokens.shape
    stored, rank, _ = adapter_down_weight.shape
    owners = lax.axis_size("dp")
    me = lax.axis_index("dp")
    side = lax.axis_index("tensor")
    share = (row_count + owners + 2) // (owners + 3)
    hot_count = HOT_PARTS * share
    down_table = adapter_down_weight.reshape(stored * rank, half_width)
    up_table = adapter_up_weight.reshape(stored * rank, -1)
    features = up_table.shape[1]

    first_piece = hot_count // 2 // 16 * 16 if hot_count >= 32 else hot_count // 2
    pieces = (first_piece, hot_count - first_piece)
    cold_send, hot_a, hot_b, place, busy = pack(
        request_adapter, adapter_slot_table, tokens, stored, owners, share, pieces
    )
    here = me.reshape(1).astype(jnp.int32)

    ring = ring_order(owners)
    to_next = [(ring[i], ring[(i + 1) % owners]) for i in range(owners)]
    to_last = [(b, a) for a, b in to_next]
    distances = [0] + [d for s in range(1, owners // 2) for d in (-s, s)] + [owners // 2]
    sources = [[0] * owners for _ in ring]
    for spot, index in enumerate(ring):
        sources[index] = [ring[(spot + d) % owners] for d in distances]
    order = lax.dynamic_index_in_dim(jnp.array(sources, jnp.int32), me, 0, keepdims=False)

    def onward(piece):
        return lax.ppermute(piece, "dp", to_next)

    def back(piece):
        return lax.ppermute(piece, "dp", to_last)

    def product(rows):
        own, local = down(here, rows, down_table, rank)
        return own, swap(own), local

    half_way = owners // 2
    group = [onward(hot_a), onward(hot_b), back(hot_a), back(hot_b)]
    base = jnp.dot(tokens, base_key_matrix, preferred_element_type=jnp.float32)
    base_own = lax.dynamic_slice_in_dim(base, side * features, features, 1)
    base_other = swap(lax.dynamic_slice_in_dim(base, (1 - side) * features, features, 1))
    cosine, sine = rope_tables(key_norm_scale.shape[0], cached_token_length)
    part = product([hot_a, hot_b])
    hot_delta = up_hot(order[:1], *part, up_table, owners, None)
    todo = [hot_delta, base]
    got = None
    for step in range(1, half_way):
        group = list(lax.optimization_barrier((*group, *todo))[:4])
        if got is None:
            cold_send = after(cold_send, group[0])
            got = lax.all_to_all(
                cold_send.reshape(owners, share, half_width + EXTRA),
                "dp",
                split_axis=0,
                concat_axis=0,
                tiled=True,
            ).reshape(owners * share, half_width + EXTRA)
        if step < half_way - 1:
            onward_group = [onward(group[0]), onward(group[1]), back(group[2]), back(group[3])]
        else:
            onward_group = [onward(group[0]), back(group[3])]
        part = product(group)
        hot_delta = up_hot(
            order[2 * step - 1 : 2 * step + 1], *part, up_table, owners, hot_delta
        )
        todo = [hot_delta]
        group = onward_group
    own, other, local = product([got])
    cold_back = lax.all_to_all(
        up_cold(own, other, local, up_table).reshape(owners, share, features),
        "dp",
        split_axis=0,
        concat_axis=0,
        tiled=True,
    ).reshape(owners * share, features)
    group = list(lax.optimization_barrier((*group, *todo))[:2])
    hot_delta = up_hot(order[owners - 1 :], *product(group), up_table, owners, hot_delta)
    hot_back = lax.all_to_all(hot_delta, "dp", split_axis=0, concat_axis=0, tiled=True)
    return finish(
        busy.reshape(1), base_own, base_other, cold_back, hot_back, place, key_norm_scale, cosine, sine
    )


def solution(mesh):
    placed = (
        P(("groups", "dp"), "tensor"),
        P("tensor", None),
        P(("groups", "dp"), None, "tensor"),
        P(("groups", "dp"), None, "tensor"),
        P(),
        P(("groups", "dp")),
        P("groups"),
        P(("groups", "dp")),
    )
    return jax.shard_map(
        on_device,
        mesh=mesh,
        in_specs=placed,
        out_specs=P(("groups", "dp"), "tensor"),
        check_vma=False,
    )
```

```python
import functools

import jax
import jax.numpy as jnp
from jax import lax
from jax.experimental import pallas as pl
from jax.experimental.pallas import tpu as pltpu
from jax.sharding import PartitionSpec as P

rope_theta = 1000000.0
LANES = 128
EXTRA = 128
HOT_PARTS = 3
ALL_VMEM = 60 * 1024 * 1024
SOME_VMEM = 16 * 1024 * 1024


def whole():
    return pl.BlockSpec(memory_space=pltpu.VMEM)


def scalars():
    return pl.BlockSpec(memory_space=pltpu.SMEM)


def params(limit=SOME_VMEM):
    return pltpu.CompilerParams(vmem_limit_bytes=limit)


def ring_order(owners):
    return [i for i in range(0, owners, 2)] + [i for i in range(owners - 1, 0, -2)]


def to_column(row):
    count = row.shape[1]
    square = lax.broadcasted_iota(jnp.int32, (count, count), 0) == lax.broadcasted_iota(
        jnp.int32, (count, count), 1
    )
    return jnp.sum(jnp.where(square, row, 0), axis=1, keepdims=True)


def choose(pick, tokens_ref, owner_row, local_row, out_ref):
    total, count = pick.shape
    width = tokens_ref.shape[1]
    out_ref[:, :width] = jnp.dot(
        pick.astype(jnp.float32).astype(jnp.bfloat16),
        tokens_ref[...],
        preferred_element_type=jnp.float32,
    ).astype(jnp.bfloat16)
    owner = jnp.sum(jnp.where(pick, owner_row + 1, 0), axis=1, keepdims=True) - 1
    local = jnp.sum(jnp.where(pick, local_row, 0), axis=1, keepdims=True)
    lane = lax.broadcasted_iota(jnp.int32, (total, EXTRA), 1)
    extra = jnp.where(lane == 0, owner, jnp.where(lane == 1, local, 0))
    out_ref[:, width:] = extra.astype(jnp.float32).astype(jnp.bfloat16)


def route_kernel(stored, owners, share, pieces, request_ref, table_ref, tokens_hbm, *refs):
    hot_refs = refs[: len(pieces)]
    place_ref, busy_ref, info_ref, tokens_ref, sem = refs[len(pieces) :]
    fetch = pltpu.make_async_copy(tokens_hbm, tokens_ref, sem)
    fetch.start()
    count = request_ref.shape[1]
    request_col = to_column(request_ref[...])
    adapters = table_ref.shape[1]
    match = request_col == lax.broadcasted_iota(jnp.int32, (count, adapters), 1)
    slot_col = jnp.sum(jnp.where(match, table_ref[...], 0), axis=1, keepdims=True)
    row_id = lax.broadcasted_iota(jnp.int32, (count, count), 0)
    col_id = lax.broadcasted_iota(jnp.int32, (count, count), 1)
    slot_row = jnp.sum(jnp.where(row_id == col_id, slot_col, 0), axis=0, keepdims=True)
    owner_col = slot_col // stored
    owner_row = slot_row // stored
    same = owner_col == owner_row
    rank_col = jnp.sum(jnp.where(same & (col_id < row_id), 1, 0), axis=1, keepdims=True)
    rank_row = jnp.sum(jnp.where(same & (row_id < col_id), 1, 0), axis=0, keepdims=True)
    cold_total = owners * share

    def place(owner, rank):
        return jnp.where(rank < share, owner * share + rank, cold_total + rank - share)

    place_ref[...] = place(owner_col, rank_col)
    busy_ref[...] = jnp.max(jnp.where(rank_row >= share, owner_row, 0), axis=1, keepdims=True)
    place_row = place(owner_row, rank_row)
    local_row = slot_row - owner_row * stored
    info_ref[0:1, :] = place_row
    info_ref[1:2, :] = owner_row
    info_ref[2:3, :] = local_row
    fetch.wait()
    first = cold_total
    for total, out_ref in zip(pieces, hot_refs):
        pick = place_row - first == lax.broadcasted_iota(jnp.int32, (total, count), 0)
        choose(pick, tokens_ref, owner_row, local_row, out_ref)
        first += total


def route(request, table, tokens, stored, owners, share, pieces):
    count, width = tokens.shape
    return pl.pallas_call(
        functools.partial(route_kernel, stored, owners, share, pieces),
        out_shape=(
            *(jax.ShapeDtypeStruct((n, width + EXTRA), jnp.bfloat16) for n in pieces),
            jax.ShapeDtypeStruct((count, 1), jnp.int32),
            jax.ShapeDtypeStruct((1, 1), jnp.int32),
            jax.ShapeDtypeStruct((3, count), jnp.int32),
        ),
        in_specs=[whole(), whole(), pl.BlockSpec(memory_space=pl.ANY)],
        out_specs=(whole(),) * (3 + len(pieces)),
        scratch_shapes=[pltpu.VMEM((count, width), jnp.bfloat16), pltpu.SemaphoreType.DMA],
        compiler_params=params(ALL_VMEM),
    )(request.reshape(1, -1), table.reshape(1, -1), tokens)


def pack_cold_kernel(info_ref, tokens_ref, out_ref):
    total, count = out_ref.shape[0], tokens_ref.shape[0]
    pick = info_ref[0:1, :] == lax.broadcasted_iota(jnp.int32, (total, count), 0)
    choose(pick, tokens_ref, info_ref[1:2, :], info_ref[2:3, :], out_ref)


def pack_cold(info, tokens, total):
    width = tokens.shape[1]
    return pl.pallas_call(
        pack_cold_kernel,
        out_shape=jax.ShapeDtypeStruct((total, width + EXTRA), jnp.bfloat16),
        in_specs=[whole(), whole()],
        out_specs=whole(),
        compiler_params=params(),
    )(info, tokens)


def down_kernel(rank, parts, me_ref, *refs):
    rows_refs = refs[:parts]
    weight_ref, out_ref, local_ref = refs[parts:]
    width = weight_ref.shape[1]
    extra = jnp.concatenate([r[:, width:].astype(jnp.float32) for r in rows_refs], axis=0).T
    local = jnp.where(extra[0:1] == me_ref[0].astype(jnp.float32), extra[1:2], -1.0)
    rows = jnp.concatenate([r[:, :width] for r in rows_refs], axis=0)
    block = 4 * rank
    out = jnp.zeros(out_ref.shape, jnp.float32)
    for first in range(0, weight_ref.shape[0], block):
        product = lax.dot_general(
            weight_ref[first : first + block, :],
            rows,
            (((1,), (1,)), ((), ())),
            preferred_element_type=jnp.float32,
        )
        for j in range(block // rank):
            mine = local == float(first // rank + j)
            out = out + jnp.where(mine, product[j * rank : (j + 1) * rank, :], 0.0)
    out_ref[...] = out
    local_ref[...] = local


def down(me, row_arrays, table, rank):
    stored_rank, width = table.shape
    count = sum(r.shape[0] for r in row_arrays)
    return pl.pallas_call(
        functools.partial(down_kernel, rank, len(row_arrays)),
        in_specs=[scalars()] + [whole()] * (len(row_arrays) + 1),
        out_specs=(whole(), whole()),
        out_shape=(
            jax.ShapeDtypeStruct((rank, count), jnp.float32),
            jax.ShapeDtypeStruct((1, count), jnp.float32),
        ),
        compiler_params=params(),
        cost_estimate=pl.CostEstimate(
            flops=2 * count * stored_rank * width,
            bytes_accessed=2 * stored_rank * width,
            transcendentals=0,
        ),
    )(me, *row_arrays, table)


def update(own_ref, other_ref, local_ref, weight_ref):
    rank, count = own_ref.shape
    pair = LANES // rank
    shrunk = (own_ref[...] + other_ref[...]).astype(jnp.bfloat16).astype(jnp.float32)
    doubled = jnp.concatenate([shrunk] * pair, axis=0).T
    local = jnp.broadcast_to(local_ref[...], (LANES, count)).T.astype(jnp.int32)
    lane_block = lax.broadcasted_iota(jnp.int32, (count, LANES), 1) // rank
    spread = jnp.concatenate(
        [
            jnp.where(lane_block + j * pair == local, doubled, 0.0).astype(jnp.bfloat16)
            for j in range(weight_ref.shape[0] // LANES)
        ],
        axis=1,
    )
    return jnp.dot(spread, weight_ref[...], preferred_element_type=jnp.float32)


def up_cold_kernel(own_ref, other_ref, local_ref, weight_ref, out_ref):
    out_ref[...] = update(own_ref, other_ref, local_ref, weight_ref).astype(jnp.bfloat16)


def up_cost(count, table):
    return pl.CostEstimate(
        flops=2 * count * table.shape[0] * table.shape[1],
        bytes_accessed=2 * table.shape[0] * table.shape[1],
        transcendentals=0,
    )


def up_cold(own, other, local, table):
    count = own.shape[1]
    return pl.pallas_call(
        up_cold_kernel,
        in_specs=[whole()] * 4,
        out_specs=whole(),
        out_shape=jax.ShapeDtypeStruct((count, table.shape[1]), jnp.bfloat16),
        compiler_params=params(),
        cost_estimate=up_cost(count, table),
    )(own, other, local, table)


def up_hot_kernel(blocks, to_ref, own_ref, other_ref, local_ref, weight_ref, *refs):
    out_ref, buffer, sems = refs[-3:]
    product = update(own_ref, other_ref, local_ref, weight_ref)
    count = buffer.shape[1]
    copies = []
    for b in range(blocks):
        buffer[b] = product[b * count : (b + 1) * count].astype(jnp.bfloat16)
        copies.append(pltpu.make_async_copy(buffer.at[b], out_ref.at[to_ref[b]], sems.at[b]))
        copies[-1].start()
    for copy in copies:
        copy.wait()


def up_hot(targets, own, other, local, table, owners, earlier):
    blocks = targets.shape[0]
    count = own.shape[1] // blocks
    kept = [] if earlier is None else [earlier]
    return pl.pallas_call(
        functools.partial(up_hot_kernel, blocks),
        in_specs=[scalars()] + [whole()] * 4 + [pl.BlockSpec(memory_space=pl.ANY) for _ in kept],
        out_specs=pl.BlockSpec(memory_space=pl.ANY),
        scratch_shapes=[
            pltpu.VMEM((blocks, count, table.shape[1]), jnp.bfloat16),
            pltpu.SemaphoreType.DMA((blocks,)),
        ],
        out_shape=jax.ShapeDtypeStruct((owners, count, table.shape[1]), jnp.bfloat16),
        input_output_aliases={5: 0} if kept else {},
        compiler_params=params(),
        cost_estimate=up_cost(blocks * count, table),
    )(targets, own, other, local, table, *kept)


def gather_kernel(own_ref, other_ref, cold_ref, place_ref, out_ref):
    count, cold_total = own_ref.shape[0], cold_ref.shape[0]
    from_cold = place_ref[...] == lax.broadcasted_iota(jnp.int32, (count, cold_total), 1)
    delta = jnp.dot(
        from_cold.astype(jnp.float32).astype(jnp.bfloat16), cold_ref[...], preferred_element_type=jnp.float32
    )
    out_ref[...] = own_ref[...] + other_ref[...] + delta


def gather_cold(own, other, cold, place):
    return pl.pallas_call(
        gather_kernel,
        in_specs=[whole()] * 4,
        out_specs=whole(),
        out_shape=jax.ShapeDtypeStruct(own.shape, jnp.float32),
        compiler_params=params(),
    )(own, other, cold, place)


def finish_kernel(
    head, first, busy_ref, keys_ref, hot_ref, place_ref, scale_ref, cos_ref, sin_ref, out_ref
):
    count, width = keys_ref.shape
    hot_total = hot_ref.shape[1]
    from_hot = place_ref[...] - first == lax.broadcasted_iota(jnp.int32, (count, hot_total), 1)
    keys = keys_ref[...] + jnp.dot(
        from_hot.astype(jnp.float32).astype(jnp.bfloat16),
        hot_ref[busy_ref[0]],
        preferred_element_type=jnp.float32,
    )
    cosine = cos_ref[...]
    sine = sin_ref[...]
    for h in range(width // head):
        one = keys[:, h * head : (h + 1) * head]
        normed = (
            one
            * lax.rsqrt(jnp.mean(one * one, axis=-1, keepdims=True) + 1e-06)
            * scale_ref[...]
        )
        turned = pltpu.roll(normed, head // 2, 1)
        out_ref[:, h * head : (h + 1) * head] = (normed * cosine + turned * sine).astype(jnp.bfloat16)


def finish(first, busy, keys, hot, place, scale, cosine, sine):
    return pl.pallas_call(
        functools.partial(finish_kernel, scale.shape[0], first),
        in_specs=[scalars()] + [whole()] * 6,
        out_specs=whole(),
        out_shape=jax.ShapeDtypeStruct(keys.shape, jnp.bfloat16),
        compiler_params=params(),
    )(busy, keys, hot, place, scale.reshape(1, -1), cosine, sine)


def after(value, *earlier):
    return lax.optimization_barrier((value,) + earlier)[0]


def rope_tables(head, cached_token_length):
    half = head // 2
    inv_freq = rope_theta ** (-(jnp.arange(half, dtype=jnp.float32) * 2.0) / head)
    angles = cached_token_length.astype(jnp.float32)[:, None] * inv_freq[None, :]
    cosine = jnp.cos(angles)
    sine = jnp.sin(angles)
    return jnp.concatenate([cosine, cosine], axis=1), jnp.concatenate([-sine, sine], axis=1)


def swap(x):
    return lax.ppermute(x, "tensor", [(0, 1), (1, 0)])


def on_device(
    tokens,
    base_key_matrix,
    adapter_down_weight,
    adapter_up_weight,
    key_norm_scale,
    request_adapter,
    adapter_slot_table,
    cached_token_length,
):
    row_count, half_width = tokens.shape
    stored, rank, _ = adapter_down_weight.shape
    owners = lax.axis_size("dp")
    me = lax.axis_index("dp")
    side = lax.axis_index("tensor")
    share = (row_count + owners + 2) // (owners + 3)
    hot_count = HOT_PARTS * share
    down_table = adapter_down_weight.reshape(stored * rank, half_width)
    up_table = adapter_up_weight.reshape(stored * rank, -1)
    features = up_table.shape[1]

    first_piece = hot_count // 2 // 16 * 16 if hot_count >= 32 else hot_count // 2
    pieces = (first_piece, hot_count - first_piece)
    hot_a, hot_b, place, busy, info = route(
        request_adapter, adapter_slot_table, tokens, stored, owners, share, pieces
    )
    cold_send = pack_cold(info, tokens, owners * share)
    here = me.reshape(1).astype(jnp.int32)

    ring = ring_order(owners)
    to_next = [(ring[i], ring[(i + 1) % owners]) for i in range(owners)]
    to_last = [(b, a) for a, b in to_next]
    distances = [0] + [d for s in range(1, owners // 2) for d in (-s, s)] + [owners // 2]
    sources = [[0] * owners for _ in ring]
    for spot, index in enumerate(ring):
        sources[index] = [ring[(spot + d) % owners] for d in distances]
    order = lax.dynamic_index_in_dim(jnp.array(sources, jnp.int32), me, 0, keepdims=False)

    def onward(piece):
        return lax.ppermute(piece, "dp", to_next)

    def back(piece):
        return lax.ppermute(piece, "dp", to_last)

    def product(rows):
        own, local = down(here, rows, down_table, rank)
        return own, swap(own), local

    def exchange(rows):
        split = rows.reshape(owners, -1, rows.shape[-1])
        return lax.all_to_all(split, "dp", split_axis=0, concat_axis=0, tiled=True).reshape(rows.shape)

    half_way = owners // 2
    group = [onward(hot_a), onward(hot_b), back(hot_a), back(hot_b)]
    got = exchange(cold_send)
    part = product([hot_a, hot_b])
    hot_delta = up_hot(order[:1], *part, up_table, owners, None)
    todo = [hot_delta]
    for step in range(1, half_way):
        group = list(lax.optimization_barrier((*group, *todo))[:4])
        if step < half_way - 1:
            following = [onward(group[0]), onward(group[1]), back(group[2]), back(group[3])]
        else:
            following = [onward(group[0]), back(group[3])]
        hot_delta = up_hot(
            order[2 * step - 1 : 2 * step + 1], *product(group), up_table, owners, hot_delta
        )
        todo = [hot_delta]
        if step == 1:
            base = jnp.dot(
                after(tokens, group[0]), base_key_matrix, preferred_element_type=jnp.float32
            )
            base_own = lax.dynamic_slice_in_dim(base, side * features, features, 1)
            base_other = swap(lax.dynamic_slice_in_dim(base, (1 - side) * features, features, 1))
            todo += [base_own]
        if step == max(half_way - 2, 1):
            cold_delta = up_cold(*product([got]), up_table)
            todo += [cold_delta]
        group = following
    cold_back = exchange(cold_delta)
    group = list(lax.optimization_barrier((*group, *todo))[:2])
    hot_delta = up_hot(order[owners - 1 :], *product(group), up_table, owners, hot_delta)
    hot_back = lax.all_to_all(hot_delta, "dp", split_axis=0, concat_axis=0, tiled=True)
    keys = gather_cold(base_own, base_other, cold_back, place)
    cosine, sine = rope_tables(key_norm_scale.shape[0], cached_token_length)
    return finish(owners * share, busy.reshape(1), keys, hot_back, place, key_norm_scale, cosine, sine)


def solution(mesh):
    placed = (
        P(("groups", "dp"), "tensor"),
        P("tensor", None),
        P(("groups", "dp"), None, "tensor"),
        P(("groups", "dp"), None, "tensor"),
        P(),
        P(("groups", "dp")),
        P("groups"),
        P(("groups", "dp")),
    )
    return jax.shard_map(
        on_device,
        mesh=mesh,
        in_specs=placed,
        out_specs=P(("groups", "dp"), "tensor"),
        check_vma=False,
    )
```

```python
import functools

import jax
import jax.numpy as jnp
from jax import lax
from jax.experimental import pallas as pl
from jax.experimental.pallas import tpu as pltpu
from jax.sharding import PartitionSpec as P

rope_theta = 1000000.0
LANES = 128
EXTRA = 128
HOT_PARTS = 3
ALL_VMEM = 60 * 1024 * 1024
LITTLE = pl.CostEstimate(flops=1, bytes_accessed=1, transcendentals=0)
SOME_VMEM = 32 * 1024 * 1024


def whole():
    return pl.BlockSpec(memory_space=pltpu.VMEM)


def scalars():
    return pl.BlockSpec(memory_space=pltpu.SMEM)


def params(limit=SOME_VMEM):
    return pltpu.CompilerParams(vmem_limit_bytes=limit)


def ring_order(owners):
    return [i for i in range(0, owners, 2)] + [i for i in range(owners - 1, 0, -2)]


def to_column(row):
    count = row.shape[1]
    square = lax.broadcasted_iota(jnp.int32, (count, count), 0) == lax.broadcasted_iota(
        jnp.int32, (count, count), 1
    )
    return jnp.sum(jnp.where(square, row, 0), axis=1, keepdims=True)


def spot_of(index, owners):
    return jnp.where(index % 2 == 0, index // 2, owners - 1 - index // 2)


def routing(pick, owner_row, local_row):
    owner = jnp.sum(jnp.where(pick, owner_row + 1, 0), axis=1, keepdims=True) - 1
    local = jnp.sum(jnp.where(pick, local_row, 0), axis=1, keepdims=True)
    lane = lax.broadcasted_iota(jnp.int32, (pick.shape[0], EXTRA), 1)
    return jnp.where(lane == 0, owner, jnp.where(lane == 1, local, 0)).astype(jnp.float32)


def route_kernel(stored, owners, share, me_ref, request_ref, table_ref, tokens_hbm, hot_ref, *refs):
    cold_refs = refs[:owners]
    place_ref, busy_ref, tokens_ref, sem = refs[owners:]
    fetch = pltpu.make_async_copy(tokens_hbm, tokens_ref, sem)
    fetch.start()
    count = request_ref.shape[1]
    request_col = to_column(request_ref[...])
    adapters = table_ref.shape[1]
    match = request_col == lax.broadcasted_iota(jnp.int32, (count, adapters), 1)
    slot_col = jnp.sum(jnp.where(match, table_ref[...], 0), axis=1, keepdims=True)
    row_id = lax.broadcasted_iota(jnp.int32, (count, count), 0)
    col_id = lax.broadcasted_iota(jnp.int32, (count, count), 1)
    slot_row = jnp.sum(jnp.where(row_id == col_id, slot_col, 0), axis=0, keepdims=True)
    owner_col = slot_col // stored
    owner_row = slot_row // stored
    same = owner_col == owner_row
    rank_col = jnp.sum(jnp.where(same & (col_id < row_id), 1, 0), axis=1, keepdims=True)
    rank_row = jnp.sum(jnp.where(same & (row_id < col_id), 1, 0), axis=0, keepdims=True)
    cold_total = owners * share

    def place(owner, rank):
        return jnp.where(rank < share, owner * share + rank, cold_total + rank - share)

    place_ref[...] = place(owner_col, rank_col)
    busy_ref[...] = jnp.max(jnp.where(rank_row >= share, owner_row, 0), axis=1, keepdims=True)
    place_row = place(owner_row, rank_row)
    local_row = slot_row - owner_row * stored
    fetch.wait()
    width = tokens_ref.shape[1]
    hot = place_row - cold_total == lax.broadcasted_iota(jnp.int32, (hot_ref.shape[0], count), 0)
    hot_ref[:, :width] = jnp.dot(
        hot.astype(jnp.float32).astype(jnp.bfloat16), tokens_ref[...], preferred_element_type=jnp.float32
    ).astype(jnp.bfloat16)
    hot_ref[:, width:] = routing(hot, owner_row, local_row).astype(jnp.bfloat16)
    distance = (spot_of(owner_row, owners) - spot_of(me_ref[0], owners) + owners) % owners
    place_row = jnp.where(rank_row < share, distance * share + rank_row, -1)
    pick = place_row == lax.broadcasted_iota(jnp.int32, (cold_total, count), 0)
    rows = jnp.dot(
        pick.astype(jnp.float32).astype(jnp.bfloat16), tokens_ref[...], preferred_element_type=jnp.float32
    )
    extra = routing(pick, owner_row, local_row)
    for k, out_ref in enumerate(cold_refs):
        out_ref[:, :width] = rows[k * share : (k + 1) * share].astype(jnp.bfloat16)
        out_ref[:, width:] = extra[k * share : (k + 1) * share].astype(jnp.bfloat16)


def route(me, request, table, tokens, stored, owners, share):
    count, width = tokens.shape
    packed = [HOT_PARTS * share] + [share] * owners
    outs = pl.pallas_call(
        functools.partial(route_kernel, stored, owners, share),
        out_shape=(
            *(jax.ShapeDtypeStruct((n, width + EXTRA), jnp.bfloat16) for n in packed),
            jax.ShapeDtypeStruct((count, 1), jnp.int32),
            jax.ShapeDtypeStruct((1, 1), jnp.int32),
        ),
        in_specs=[scalars(), whole(), whole(), pl.BlockSpec(memory_space=pl.ANY)],
        out_specs=(whole(),) * (len(packed) + 2),
        scratch_shapes=[pltpu.VMEM((count, width), jnp.bfloat16), pltpu.SemaphoreType.DMA],
        compiler_params=params(ALL_VMEM),
    )(me, request.reshape(1, -1), table.reshape(1, -1), tokens)
    return outs[0], outs[1 : owners + 1], outs[-2], outs[-1]


def fetch_rows(source, target, sems):
    pieces = sems.shape[0]
    size = source.shape[0] // pieces
    copies = []
    for k in range(pieces):
        part = pl.ds(k * size, size)
        copies.append(pltpu.make_async_copy(source.at[part], target.at[part], sems.at[k]))
        copies[-1].start()
    return copies, size


def base_kernel(side_ref, tokens_ref, weight_hbm, own_ref, other_ref, weight, sems):
    half = own_ref.shape[1]
    copies, size = fetch_rows(weight_hbm, weight, sems)
    total = None
    for k, copy in enumerate(copies):
        copy.wait()
        part = jnp.dot(
            tokens_ref[:, k * size : (k + 1) * size],
            weight[k * size : (k + 1) * size, :],
            preferred_element_type=jnp.float32,
        )
        total = part if total is None else total + part

    @pl.when(side_ref[0] == 0)
    def _():
        own_ref[...] = total[:, :half]
        other_ref[...] = total[:, half:]

    @pl.when(side_ref[0] != 0)
    def _():
        own_ref[...] = total[:, half:]
        other_ref[...] = total[:, :half]


def base_product(side, tokens, weight):
    half = jax.ShapeDtypeStruct((tokens.shape[0], weight.shape[1] // 2), jnp.float32)
    return pl.pallas_call(
        base_kernel,
        in_specs=[scalars(), whole(), pl.BlockSpec(memory_space=pltpu.HBM)],
        out_specs=(whole(), whole()),
        out_shape=(half, half),
        scratch_shapes=[pltpu.VMEM(weight.shape, weight.dtype), pltpu.SemaphoreType.DMA((5,))],
        compiler_params=params(),
        cost_estimate=LITTLE,
    )(side, tokens, weight)


def keep_kernel(table_ref, out_ref, sem):
    copy = pltpu.make_async_copy(table_ref, out_ref, sem)
    copy.start()
    copy.wait()


def keep(table):
    return pl.pallas_call(
        keep_kernel,
        in_specs=[pl.BlockSpec(memory_space=pl.ANY)],
        out_specs=whole(),
        out_shape=pltpu.VMEM(table.shape, table.dtype),
        scratch_shapes=[pltpu.SemaphoreType.DMA],
        compiler_params=params(),
        cost_estimate=LITTLE,
    )(table)


def down_kernel(rank, parts, me_ref, *refs):
    rows_refs = refs[:parts]
    weight_ref, out_ref, local_ref = refs[parts:]
    width = weight_ref.shape[1]
    extra = jnp.concatenate([r[:, width:].astype(jnp.float32) for r in rows_refs], axis=0).T
    local = jnp.where(extra[0:1] == me_ref[0].astype(jnp.float32), extra[1:2], -1.0)
    rows = jnp.concatenate([r[:, :width] for r in rows_refs], axis=0)
    block = 4 * rank
    out = jnp.zeros(out_ref.shape, jnp.float32)
    for first in range(0, weight_ref.shape[0], block):
        product = lax.dot_general(
            weight_ref[first : first + block, :],
            rows,
            (((1,), (1,)), ((), ())),
            preferred_element_type=jnp.float32,
        )
        for j in range(block // rank):
            mine = local == float(first // rank + j)
            out = out + jnp.where(mine, product[j * rank : (j + 1) * rank, :], 0.0)
    out_ref[...] = out
    local_ref[...] = local


def down(me, row_arrays, table, rank):
    count = sum(r.shape[0] for r in row_arrays)
    return pl.pallas_call(
        functools.partial(down_kernel, rank, len(row_arrays)),
        in_specs=[scalars()] + [whole()] * (len(row_arrays) + 1),
        out_specs=(whole(), whole()),
        out_shape=(
            jax.ShapeDtypeStruct((rank, count), jnp.float32),
            jax.ShapeDtypeStruct((1, count), jnp.float32),
        ),
        compiler_params=params(),
        cost_estimate=LITTLE,
    )(me, *row_arrays, table)


def update(own_ref, other_ref, local_ref, weight_ref):
    rank, count = own_ref.shape
    pair = LANES // rank
    shrunk = (own_ref[...] + other_ref[...]).astype(jnp.bfloat16).astype(jnp.float32)
    doubled = jnp.concatenate([shrunk] * pair, axis=0).T
    local = jnp.broadcast_to(local_ref[...], (LANES, count)).T.astype(jnp.int32)
    lane_block = lax.broadcasted_iota(jnp.int32, (count, LANES), 1) // rank
    spread = jnp.concatenate(
        [
            jnp.where(lane_block + j * pair == local, doubled, 0.0).astype(jnp.bfloat16)
            for j in range(weight_ref.shape[0] // LANES)
        ],
        axis=1,
    )
    return jnp.dot(spread, weight_ref[...], preferred_element_type=jnp.float32)


def up_kernel(units, kept, to_ref, own_ref, other_ref, local_ref, weight_ref, *refs):
    out_ref, buffer, sems = refs[kept:]
    product = update(own_ref, other_ref, local_ref, weight_ref)
    share, features = buffer.shape[1:]
    copies = []
    for k, (place, column) in enumerate(units):
        buffer[k] = product[k * share : (k + 1) * share].astype(jnp.bfloat16)
        target = out_ref.at[to_ref[place], :, pl.ds(column * features, features)]
        copies.append(pltpu.make_async_copy(buffer.at[k], target, sems.at[k]))
        copies[-1].start()
    for copy in copies:
        copy.wait()


def up(targets, units, own, other, local, table, out):
    given = [] if isinstance(out, jax.ShapeDtypeStruct) else [out]
    anywhere = pl.BlockSpec(memory_space=pl.ANY)
    share = own.shape[1] // len(units)
    return pl.pallas_call(
        functools.partial(up_kernel, units, len(given)),
        in_specs=[scalars()] + [whole()] * 4 + [anywhere] * len(given),
        out_specs=anywhere,
        scratch_shapes=[
            pltpu.VMEM((len(units), share, table.shape[1]), jnp.bfloat16),
            pltpu.SemaphoreType.DMA((len(units),)),
        ],
        out_shape=jax.ShapeDtypeStruct(out.shape, jnp.bfloat16),
        input_output_aliases={5: 0} if given else {},
        compiler_params=params(),
        cost_estimate=LITTLE,
    )(targets, own, other, local, table, *given)


def finish_kernel(
    head, busy_ref, own_ref, other_ref, back_ref, place_ref, scale_ref, cos_ref, sin_ref, out_ref
):
    count, width = own_ref.shape
    owners, share, _ = back_ref.shape
    pieces = [back_ref[o, :, HOT_PARTS * width :].astype(jnp.float32) for o in range(owners)]
    pieces += [
        back_ref[busy_ref[0], :, c * width : (c + 1) * width].astype(jnp.float32)
        for c in range(HOT_PARTS)
    ]
    back = jnp.concatenate(pieces, axis=0).astype(jnp.bfloat16)
    chosen = place_ref[...] == lax.broadcasted_iota(jnp.int32, (count, back.shape[0]), 1)
    keys = (own_ref[...] + other_ref[...]) + jnp.dot(
        chosen.astype(jnp.float32).astype(jnp.bfloat16), back, preferred_element_type=jnp.float32
    )
    cosine = cos_ref[...]
    sine = sin_ref[...]
    for h in range(width // head):
        one = keys[:, h * head : (h + 1) * head]
        normed = (
            one
            * lax.rsqrt(jnp.mean(one * one, axis=-1, keepdims=True) + 1e-06)
            * scale_ref[...]
        )
        turned = pltpu.roll(normed, head // 2, 1)
        out_ref[:, h * head : (h + 1) * head] = (normed * cosine + turned * sine).astype(jnp.bfloat16)


def finish(busy, own, other, back, place, scale, cosine, sine):
    return pl.pallas_call(
        functools.partial(finish_kernel, scale.shape[0]),
        in_specs=[scalars()] + [whole()] * 7,
        out_specs=whole(),
        out_shape=jax.ShapeDtypeStruct(own.shape, jnp.bfloat16),
        compiler_params=params(),
    )(busy, own, other, back, place, scale.reshape(1, -1), cosine, sine)


def after(value, *earlier):
    return lax.optimization_barrier((value,) + earlier)[0]


def rope_tables(head, cached_token_length):
    half = head // 2
    inv_freq = rope_theta ** (-(jnp.arange(half, dtype=jnp.float32) * 2.0) / head)
    angles = cached_token_length.astype(jnp.float32)[:, None] * inv_freq[None, :]
    cosine = jnp.cos(angles)
    sine = jnp.sin(angles)
    return jnp.concatenate([cosine, cosine], axis=1), jnp.concatenate([-sine, sine], axis=1)


def swap(x):
    return lax.ppermute(x, "tensor", [(0, 1), (1, 0)])


def on_device(
    tokens,
    base_key_matrix,
    adapter_down_weight,
    adapter_up_weight,
    key_norm_scale,
    request_adapter,
    adapter_slot_table,
    cached_token_length,
):
    row_count, half_width = tokens.shape
    stored, rank, _ = adapter_down_weight.shape
    owners = lax.axis_size("dp")
    me = lax.axis_index("dp")
    side = lax.axis_index("tensor")
    share = (row_count + owners + 2) // (owners + 3)
    hot_count = HOT_PARTS * share
    down_table = adapter_down_weight.reshape(stored * rank, half_width)
    up_table = adapter_up_weight.reshape(stored * rank, -1)
    features = up_table.shape[1]

    here = me.reshape(1).astype(jnp.int32)
    hot, cold, place, busy = route(
        here, request_adapter, adapter_slot_table, tokens, stored, owners, share
    )

    ring = ring_order(owners)
    half_way = owners // 2

    def along(rows, distance):
        return lax.ppermute(
            rows, "dp", [(ring[i], ring[(i + distance) % owners]) for i in range(owners)]
        )

    distances = [0] + [d for s in range(1, half_way) for d in (s, -s)] + [half_way]
    sources = [[0] * (2 * owners) for _ in ring]
    for spot, index in enumerate(ring):
        sources[index] = [ring[(spot - d) % owners] for d in distances + list(range(owners))]
    order = lax.dynamic_index_in_dim(jnp.array(sources, jnp.int32), me, 0, keepdims=False)

    def product(rows):
        own, local = down(here, rows, down_table, rank)
        return own, swap(own), local

    group = [along(hot, 1), along(hot, -1)]
    waves = {d: [d, owners - d] for d in range(1, half_way)}
    waves[1] = waves[1] + [half_way]
    got = {0: cold[0]}
    for d in waves[1]:
        got[d] = along(cold[d], d)
    cut = hot_count // 2 // 16 * 16 if hot_count >= 32 else hot_count // 2

    def hot_units(first, blocks):
        return [(first + k, column) for k in range(blocks) for column in range(HOT_PARTS)]

    def cold_units(chosen):
        return [(owners + d, HOT_PARTS) for d in chosen]

    delta = jax.ShapeDtypeStruct((owners, share, (HOT_PARTS + 1) * features), jnp.bfloat16)
    down_table = keep(down_table)
    todo = [got[d] for d in waves[1]] + [down_table]
    for step in range(1, half_way):
        group = list(lax.optimization_barrier((*group, *todo))[:2])
        if step < half_way - 1:
            following = [along(group[0], 1), along(group[1], -1)]
            for d in waves[step + 1]:
                got[d] = along(after(cold[d], group[0]), d)
        else:
            following = [along(group[0][:cut], 1), along(group[1][cut:], -1)]
        rows, units = list(group), hot_units(2 * step - 1, 2)
        if step == 1:
            rows, units = [hot] + rows, hot_units(0, 3)
        if step == half_way - 2:
            chosen = [d for d in range(owners) if d not in waves[half_way - 1]]
        elif step == half_way - 1:
            chosen = waves[step]
        else:
            chosen = []
        rows += [got[d] for d in chosen]
        rows = lax.optimization_barrier((*rows, group[0]))[:-1]
        delta = up(order, units + cold_units(chosen), *product(list(rows)), up_table, delta)
        todo = [delta] + [got[d] for d in waves.get(step + 1, [])]
        group = following
    group = list(lax.optimization_barrier((*group, delta))[:2])
    last = product(group)
    delta = up(order, hot_units(owners - 1, 1), *last, up_table, delta)
    back = lax.all_to_all(delta, "dp", split_axis=0, concat_axis=0, tiled=True)
    base_own, base_give = base_product(
        side.reshape(1).astype(jnp.int32), after(tokens, last[0]), base_key_matrix
    )
    cosine, sine = rope_tables(key_norm_scale.shape[0], cached_token_length)
    return finish(
        busy.reshape(1), base_own, swap(base_give), back, place, key_norm_scale, cosine, sine
    )


def solution(mesh):
    placed = (
        P(("groups", "dp"), "tensor"),
        P("tensor", None),
        P(("groups", "dp"), None, "tensor"),
        P(("groups", "dp"), None, "tensor"),
        P(),
        P(("groups", "dp")),
        P("groups"),
        P(("groups", "dp")),
    )
    return jax.shard_map(
        on_device,
        mesh=mesh,
        in_specs=placed,
        out_specs=P(("groups", "dp"), "tensor"),
        check_vma=False,
    )
```

```python
import functools

import jax
import jax.numpy as jnp
from jax import lax
from jax.experimental import pallas as pl
from jax.experimental.pallas import tpu as pltpu
from jax.sharding import PartitionSpec as P

rope_theta = 1000000.0
LANES = 128
EXTRA = 128
HOT_PARTS = 3
ALL_VMEM = 60 * 1024 * 1024
LITTLE = pl.CostEstimate(flops=1, bytes_accessed=1, transcendentals=0)
SOME_VMEM = 32 * 1024 * 1024


def whole():
    return pl.BlockSpec(memory_space=pltpu.VMEM)


def scalars():
    return pl.BlockSpec(memory_space=pltpu.SMEM)


def params(limit=SOME_VMEM):
    return pltpu.CompilerParams(vmem_limit_bytes=limit)


def ring_order(owners):
    return [i for i in range(0, owners, 2)] + [i for i in range(owners - 1, 0, -2)]


def to_column(row):
    count = row.shape[1]
    square = lax.broadcasted_iota(jnp.int32, (count, count), 0) == lax.broadcasted_iota(
        jnp.int32, (count, count), 1
    )
    return jnp.sum(jnp.where(square, row, 0), axis=1, keepdims=True)


def spot_of(index, owners):
    return jnp.where(index % 2 == 0, index // 2, owners - 1 - index // 2)


def route_kernel(stored, owners, share, me_ref, request_ref, table_ref, tokens_hbm, hot_ref, *refs):
    cold_refs = refs[:owners]
    place_ref, busy_ref, tokens_ref, sem = refs[owners:]
    fetch = pltpu.make_async_copy(tokens_hbm, tokens_ref, sem)
    fetch.start()
    count = request_ref.shape[1]
    adapters = table_ref.shape[1]
    table_col = to_column(table_ref[...])
    match = request_ref[...] == lax.broadcasted_iota(jnp.int32, (adapters, count), 0)
    slot_row = jnp.sum(jnp.where(match, table_col, 0), axis=0, keepdims=True)
    slot_col = to_column(slot_row)
    owner_col = slot_col // stored
    owner_row = slot_row // stored
    row_id = lax.broadcasted_iota(jnp.int32, (count, count), 0)
    col_id = lax.broadcasted_iota(jnp.int32, (count, count), 1)
    earlier = (owner_col == owner_row) & (row_id < col_id)
    rank_row = jnp.sum(jnp.where(earlier, 1, 0), axis=0, keepdims=True)
    cold_total = owners * share
    place_ref[...] = jnp.where(
        rank_row < share, owner_row * share + rank_row, cold_total + rank_row - share
    )
    busy_ref[...] = jnp.max(jnp.where(rank_row >= share, owner_row, 0), axis=1, keepdims=True)
    distance = (spot_of(owner_row, owners) - spot_of(me_ref[0], owners) + owners) % owners
    position = jnp.where(rank_row < share, distance * share, cold_total - share) + rank_row
    total = cold_total + hot_ref.shape[0]
    pick = position == lax.broadcasted_iota(jnp.int32, (total, count), 0)
    pick = pick.astype(jnp.float32).astype(jnp.bfloat16)
    lane = lax.broadcasted_iota(jnp.int32, (count, EXTRA), 1)
    beside = jnp.where(lane == 0, owner_col + 1, jnp.where(lane == 1, slot_col - owner_col * stored, 0))
    beside = beside.astype(jnp.float32).astype(jnp.bfloat16)
    width = tokens_ref.shape[1]
    extra = jnp.dot(pick, beside, preferred_element_type=jnp.float32)
    fetch.wait()
    rows = jnp.dot(pick, tokens_ref[...], preferred_element_type=jnp.float32)
    firsts = [cold_total] + [k * share for k in range(owners)]
    for first, out_ref in zip(firsts, (hot_ref, *cold_refs)):
        size = out_ref.shape[0]
        out_ref[:, :width] = rows[first : first + size].astype(jnp.bfloat16)
        out_ref[:, width:] = extra[first : first + size].astype(jnp.bfloat16)


def route(me, request, table, tokens, stored, owners, share):
    count, width = tokens.shape
    packed = [HOT_PARTS * share] + [share] * owners
    outs = pl.pallas_call(
        functools.partial(route_kernel, stored, owners, share),
        out_shape=(
            *(jax.ShapeDtypeStruct((n, width + EXTRA), jnp.bfloat16) for n in packed),
            jax.ShapeDtypeStruct((1, count), jnp.int32),
            jax.ShapeDtypeStruct((1, 1), jnp.int32),
        ),
        in_specs=[scalars(), whole(), whole(), pl.BlockSpec(memory_space=pl.ANY)],
        out_specs=(whole(),) * (len(packed) + 2),
        scratch_shapes=[pltpu.VMEM((count, width), jnp.bfloat16), pltpu.SemaphoreType.DMA],
        compiler_params=params(ALL_VMEM),
    )(me, request.reshape(1, -1), table.reshape(1, -1), tokens)
    return outs[0], outs[1 : owners + 1], outs[-2], outs[-1]


def fetch_rows(source, target, sems):
    pieces = sems.shape[0]
    size = source.shape[0] // pieces
    copies = []
    for k in range(pieces):
        part = pl.ds(k * size, size)
        copies.append(pltpu.make_async_copy(source.at[part], target.at[part], sems.at[k]))
        copies[-1].start()
    return copies, size


def base_kernel(side_ref, tokens_ref, place_ref, weight_hbm, own_ref, other_ref, column_ref, weight, sems):
    half = own_ref.shape[1]
    copies, size = fetch_rows(weight_hbm, weight, sems)
    column_ref[...] = to_column(place_ref[...])
    total = None
    for k, copy in enumerate(copies):
        copy.wait()
        part = jnp.dot(
            tokens_ref[:, k * size : (k + 1) * size],
            weight[k * size : (k + 1) * size, :],
            preferred_element_type=jnp.float32,
        )
        total = part if total is None else total + part

    @pl.when(side_ref[0] == 0)
    def _():
        own_ref[...] = total[:, :half]
        other_ref[...] = total[:, half:]

    @pl.when(side_ref[0] != 0)
    def _():
        own_ref[...] = total[:, half:]
        other_ref[...] = total[:, :half]


def base_product(side, tokens, place, weight):
    column = jax.ShapeDtypeStruct((tokens.shape[0], 1), jnp.int32)
    half = jax.ShapeDtypeStruct((tokens.shape[0], weight.shape[1] // 2), jnp.float32)
    return pl.pallas_call(
        base_kernel,
        in_specs=[scalars(), whole(), whole(), pl.BlockSpec(memory_space=pltpu.HBM)],
        out_specs=(whole(),) * 3,
        out_shape=(half, half, column),
        scratch_shapes=[pltpu.VMEM(weight.shape, weight.dtype), pltpu.SemaphoreType.DMA((5,))],
        compiler_params=params(),
        cost_estimate=LITTLE,
    )(side, tokens, place, weight)


def keep_kernel(table_ref, out_ref, sem):
    copy = pltpu.make_async_copy(table_ref, out_ref, sem)
    copy.start()
    copy.wait()


def keep(table):
    return pl.pallas_call(
        keep_kernel,
        in_specs=[pl.BlockSpec(memory_space=pl.ANY)],
        out_specs=whole(),
        out_shape=pltpu.VMEM(table.shape, table.dtype),
        scratch_shapes=[pltpu.SemaphoreType.DMA],
        compiler_params=params(),
        cost_estimate=LITTLE,
    )(table)


def down_kernel(rank, parts, me_ref, *refs):
    rows_refs = refs[:parts]
    weight_ref, out_ref, local_ref = refs[parts:]
    width = weight_ref.shape[1]
    extra = jnp.concatenate([r[:, width:].astype(jnp.float32) for r in rows_refs], axis=0).T
    local = jnp.where(extra[0:1] == (me_ref[0] + 1).astype(jnp.float32), extra[1:2], -1.0)
    rows = jnp.concatenate([r[:, :width] for r in rows_refs], axis=0)
    block = 4 * rank
    out = jnp.zeros(out_ref.shape, jnp.float32)
    for first in range(0, weight_ref.shape[0], block):
        product = lax.dot_general(
            weight_ref[first : first + block, :],
            rows,
            (((1,), (1,)), ((), ())),
            preferred_element_type=jnp.float32,
        )
        for j in range(block // rank):
            mine = local == float(first // rank + j)
            out = out + jnp.where(mine, product[j * rank : (j + 1) * rank, :], 0.0)
    out_ref[...] = out
    local_ref[...] = local


def down(me, row_arrays, table, rank):
    count = sum(r.shape[0] for r in row_arrays)
    return pl.pallas_call(
        functools.partial(down_kernel, rank, len(row_arrays)),
        in_specs=[scalars()] + [whole()] * (len(row_arrays) + 1),
        out_specs=(whole(), whole()),
        out_shape=(
            jax.ShapeDtypeStruct((rank, count), jnp.float32),
            jax.ShapeDtypeStruct((1, count), jnp.float32),
        ),
        compiler_params=params(),
        cost_estimate=LITTLE,
    )(me, *row_arrays, table)


def update(own_ref, other_ref, local_ref, weight_ref):
    rank, count = own_ref.shape
    pair = LANES // rank
    shrunk = (own_ref[...] + other_ref[...]).astype(jnp.bfloat16).astype(jnp.float32)
    doubled = jnp.concatenate([shrunk] * pair, axis=0).T
    local = jnp.broadcast_to(local_ref[...], (LANES, count)).T.astype(jnp.int32)
    lane_block = lax.broadcasted_iota(jnp.int32, (count, LANES), 1) // rank
    spread = jnp.concatenate(
        [
            jnp.where(lane_block + j * pair == local, doubled, 0.0).astype(jnp.bfloat16)
            for j in range(weight_ref.shape[0] // LANES)
        ],
        axis=1,
    )
    return jnp.dot(spread, weight_ref[...], preferred_element_type=jnp.float32)


def up_kernel(units, kept, to_ref, own_ref, other_ref, local_ref, weight_ref, *refs):
    out_ref, buffer, sems = refs[kept:]
    product = update(own_ref, other_ref, local_ref, weight_ref)
    share, features = buffer.shape[1:]
    copies = []
    for k, (place, column) in enumerate(units):
        buffer[k] = product[k * share : (k + 1) * share].astype(jnp.bfloat16)
        target = out_ref.at[to_ref[place], :, pl.ds(column * features, features)]
        copies.append(pltpu.make_async_copy(buffer.at[k], target, sems.at[k]))
        copies[-1].start()
    for copy in copies:
        copy.wait()


def up(targets, units, own, other, local, table, out):
    given = [] if isinstance(out, jax.ShapeDtypeStruct) else [out]
    anywhere = pl.BlockSpec(memory_space=pl.ANY)
    share = own.shape[1] // len(units)
    return pl.pallas_call(
        functools.partial(up_kernel, units, len(given)),
        in_specs=[scalars()] + [whole()] * 4 + [anywhere] * len(given),
        out_specs=anywhere,
        scratch_shapes=[
            pltpu.VMEM((len(units), share, table.shape[1]), jnp.bfloat16),
            pltpu.SemaphoreType.DMA((len(units),)),
        ],
        out_shape=jax.ShapeDtypeStruct(out.shape, jnp.bfloat16),
        input_output_aliases={5: 0} if given else {},
        compiler_params=params(),
        cost_estimate=LITTLE,
    )(targets, own, other, local, table, *given)


def finish_kernel(
    head, busy_ref, far_ref, own_ref, other_ref, back_ref, last_ref, place_ref, scale_ref, cos_ref, sin_ref, out_ref
):
    count, width = own_ref.shape
    owners, share, _ = back_ref.shape
    pieces = [back_ref[o, :, HOT_PARTS * width :].astype(jnp.float32) for o in range(owners)]
    from_far = busy_ref[0] == far_ref[0]
    for c in range(HOT_PARTS):
        columns = slice(c * width, (c + 1) * width)
        near = back_ref[busy_ref[0], :, columns].astype(jnp.float32)
        pieces.append(jnp.where(from_far, last_ref[0, :, columns].astype(jnp.float32), near))
    back = jnp.concatenate(pieces, axis=0).astype(jnp.bfloat16)
    chosen = place_ref[...] == lax.broadcasted_iota(jnp.int32, (count, back.shape[0]), 1)
    keys = (own_ref[...] + other_ref[...]) + jnp.dot(
        chosen.astype(jnp.float32).astype(jnp.bfloat16), back, preferred_element_type=jnp.float32
    )
    cosine = cos_ref[...]
    sine = sin_ref[...]
    for h in range(width // head):
        one = keys[:, h * head : (h + 1) * head]
        normed = (
            one
            * lax.rsqrt(jnp.mean(one * one, axis=-1, keepdims=True) + 1e-06)
            * scale_ref[...]
        )
        turned = pltpu.roll(normed, head // 2, 1)
        out_ref[:, h * head : (h + 1) * head] = (normed * cosine + turned * sine).astype(jnp.bfloat16)


def finish(busy, far, own, other, back, last, place, scale, cosine, sine):
    return pl.pallas_call(
        functools.partial(finish_kernel, scale.shape[0]),
        in_specs=[scalars()] * 2 + [whole()] * 8,
        out_specs=whole(),
        out_shape=jax.ShapeDtypeStruct(own.shape, jnp.bfloat16),
        compiler_params=params(),
    )(busy, far, own, other, back, last, place, scale.reshape(1, -1), cosine, sine)


def after(value, *earlier):
    return lax.optimization_barrier((value,) + earlier)[0]


def rope_tables(head, cached_token_length):
    half = head // 2
    inv_freq = rope_theta ** (-(jnp.arange(half, dtype=jnp.float32) * 2.0) / head)
    angles = cached_token_length.astype(jnp.float32)[:, None] * inv_freq[None, :]
    cosine = jnp.cos(angles)
    sine = jnp.sin(angles)
    return jnp.concatenate([cosine, cosine], axis=1), jnp.concatenate([-sine, sine], axis=1)


def swap(x):
    return lax.ppermute(x, "tensor", [(0, 1), (1, 0)])


def on_device(
    tokens,
    base_key_matrix,
    adapter_down_weight,
    adapter_up_weight,
    key_norm_scale,
    request_adapter,
    adapter_slot_table,
    cached_token_length,
):
    row_count, half_width = tokens.shape
    stored, rank, _ = adapter_down_weight.shape
    owners = lax.axis_size("dp")
    me = lax.axis_index("dp")
    side = lax.axis_index("tensor")
    share = (row_count + owners + 2) // (owners + 3)
    hot_count = HOT_PARTS * share
    down_table = adapter_down_weight.reshape(stored * rank, half_width)
    up_table = adapter_up_weight.reshape(stored * rank, -1)
    features = up_table.shape[1]

    here = me.reshape(1).astype(jnp.int32)
    hot, cold, place, busy = route(
        here, request_adapter, adapter_slot_table, tokens, stored, owners, share
    )

    ring = ring_order(owners)
    half_way = owners // 2

    def along(rows, distance):
        return lax.ppermute(
            rows, "dp", [(ring[i], ring[(i + distance) % owners]) for i in range(owners)]
        )

    distances = [0] + [d for s in range(1, half_way) for d in (s, -s)] + [half_way]
    sources = [[0] * (2 * owners) for _ in ring]
    for spot, index in enumerate(ring):
        sources[index] = [ring[(spot - d) % owners] for d in distances + list(range(owners))]
    order = lax.dynamic_index_in_dim(jnp.array(sources, jnp.int32), me, 0, keepdims=False)

    def product(rows):
        own, local = down(here, rows, down_table, rank)
        return own, swap(own), local

    group = [along(hot, 1), along(hot, -1)]
    waves = {d: [d, owners - d] for d in range(1, half_way)}
    waves[half_way - 1] = waves[half_way - 1] + [half_way]
    got = {0: cold[0]}
    for d in waves[1]:
        got[d] = along(cold[d], d)
    cut = hot_count // 2 // 16 * 16 if hot_count >= 32 else hot_count // 2

    def hot_units(first, blocks):
        return [(first + k, column) for k in range(blocks) for column in range(HOT_PARTS)]

    def cold_units(chosen):
        return [(owners + d, HOT_PARTS) for d in chosen]

    delta = jax.ShapeDtypeStruct((owners, share, (HOT_PARTS + 1) * features), jnp.bfloat16)
    down_table = keep(down_table)
    todo = [got[d] for d in waves[1]] + [down_table]
    for step in range(1, half_way):
        group = list(lax.optimization_barrier((*group, *todo))[:2])
        if step < half_way - 1:
            following = [along(group[0], 1), along(group[1], -1)]
            for d in waves[step + 1]:
                got[d] = along(after(cold[d], group[0]), d)
        else:
            following = [along(group[0][:cut], 1), along(group[1][cut:], -1)]
        rows, units = list(group), hot_units(2 * step - 1, 2)
        if step == 1:
            rows, units = [hot] + rows, hot_units(0, 3)
        if step == half_way - 2:
            chosen = [d for d in range(owners) if d not in waves[half_way - 1]]
        elif step == half_way - 1:
            chosen = waves[step]
        else:
            chosen = []
        rows += [got[d] for d in chosen]
        rows = lax.optimization_barrier((*rows, group[0]))[:-1]
        delta = up(order, units + cold_units(chosen), *product(list(rows)), up_table, delta)
        todo = [delta] + [got[d] for d in waves.get(step + 1, [])]
        group = following
    *group, delta = lax.optimization_barrier((*group, delta))
    back = lax.all_to_all(delta, "dp", split_axis=0, concat_axis=0, tiled=True)
    last = product(group)
    far_delta = jax.ShapeDtypeStruct((1, share, HOT_PARTS * features), jnp.bfloat16)
    far_delta = up(
        jnp.zeros((1,), jnp.int32), [(0, c) for c in range(HOT_PARTS)], *last, up_table, far_delta
    )
    tokens = after(tokens, far_delta)
    far_delta = along(far_delta, half_way)
    base_own, base_give, place = base_product(
        side.reshape(1).astype(jnp.int32), tokens, place, base_key_matrix
    )
    cosine, sine = rope_tables(key_norm_scale.shape[0], cached_token_length)
    return finish(
        busy.reshape(1),
        order[owners - 1 : owners],
        base_own,
        swap(base_give),
        back,
        far_delta,
        place,
        key_norm_scale,
        cosine,
        sine,
    )


def solution(mesh):
    placed = (
        P(("groups", "dp"), "tensor"),
        P("tensor", None),
        P(("groups", "dp"), None, "tensor"),
        P(("groups", "dp"), None, "tensor"),
        P(),
        P(("groups", "dp")),
        P("groups"),
        P(("groups", "dp")),
    )
    return jax.shard_map(
        on_device,
        mesh=mesh,
        in_specs=placed,
        out_specs=P(("groups", "dp"), "tensor"),
        check_vma=False,
    )
```

```python
import functools

import jax
import jax.numpy as jnp
from jax import lax
from jax.experimental import pallas as pl
from jax.experimental.pallas import tpu as pltpu
from jax.sharding import PartitionSpec as P

rope_theta = 1000000.0
LANES = 128
EXTRA = 128
COLD, HOT, REST = 0, 1, 2
HOT_PARTS = 3
ALL_VMEM = 60 * 1024 * 1024
LITTLE = pl.CostEstimate(flops=1, bytes_accessed=1, transcendentals=0)
SOME_VMEM = 32 * 1024 * 1024


def whole():
    return pl.BlockSpec(memory_space=pltpu.VMEM)


def scalars():
    return pl.BlockSpec(memory_space=pltpu.SMEM)


def params(limit=SOME_VMEM):
    return pltpu.CompilerParams(vmem_limit_bytes=limit)


def ring_order(owners):
    return [i for i in range(0, owners, 2)] + [i for i in range(owners - 1, 0, -2)]


def to_column(row):
    count = row.shape[1]
    square = lax.broadcasted_iota(jnp.int32, (count, count), 0) == lax.broadcasted_iota(
        jnp.int32, (count, count), 1
    )
    return jnp.sum(jnp.where(square, row, 0), axis=1, keepdims=True)


def spot_of(index, owners):
    return jnp.where(index % 2 == 0, index // 2, owners - 1 - index // 2)


def route_kernel(stored, owners, share, me_ref, request_ref, table_ref, tokens_hbm, hot_ref, *refs):
    cold_refs = refs[:owners]
    place_ref, busy_ref, tokens_ref, sem = refs[owners:]
    fetch = pltpu.make_async_copy(tokens_hbm, tokens_ref, sem)
    fetch.start()
    count = request_ref.shape[1]
    adapters = table_ref.shape[1]
    table_col = to_column(table_ref[...])
    match = request_ref[...] == lax.broadcasted_iota(jnp.int32, (adapters, count), 0)
    slot_row = jnp.sum(jnp.where(match, table_col, 0), axis=0, keepdims=True)
    slot_col = to_column(slot_row)
    owner_col = slot_col // stored
    owner_row = slot_row // stored
    row_id = lax.broadcasted_iota(jnp.int32, (count, count), 0)
    col_id = lax.broadcasted_iota(jnp.int32, (count, count), 1)
    earlier = (owner_col == owner_row) & (row_id < col_id)
    rank_row = jnp.sum(jnp.where(earlier, 1, 0), axis=0, keepdims=True)
    cold_total = owners * share
    place_ref[...] = jnp.where(
        rank_row < share, owner_row * share + rank_row, cold_total + rank_row - share
    )
    busy_ref[...] = jnp.max(jnp.where(rank_row >= share, owner_row, 0), axis=1, keepdims=True)
    distance = (spot_of(owner_row, owners) - spot_of(me_ref[0], owners) + owners) % owners
    position = jnp.where(rank_row < share, distance * share, cold_total - share) + rank_row
    total = cold_total + hot_ref.shape[0]
    pick = position == lax.broadcasted_iota(jnp.int32, (total, count), 0)
    pick = pick.astype(jnp.float32).astype(jnp.bfloat16)
    lane = lax.broadcasted_iota(jnp.int32, (count, EXTRA), 1)
    local_col = slot_col - owner_col * stored

    def beside(pick, first):
        codes = jnp.where(lane == first, owner_col + 1, jnp.where(lane == first + 1, local_col, 0))
        codes = codes.astype(jnp.float32).astype(jnp.bfloat16)
        return jnp.dot(pick, codes, preferred_element_type=jnp.float32)

    hot_extra = jnp.zeros((share, EXTRA), jnp.float32)
    for part in range(HOT_PARTS):
        piece = position - (cold_total + part * share) == lax.broadcasted_iota(
            jnp.int32, (share, count), 0
        )
        hot_extra = hot_extra + beside(piece.astype(jnp.float32).astype(jnp.bfloat16), 2 + 2 * part)
    width = tokens_ref.shape[1]
    extra = beside(pick, 0)
    fetch.wait()
    rows = jnp.dot(pick, tokens_ref[...], preferred_element_type=jnp.float32)
    hot_ref[...] = rows[cold_total:].astype(jnp.bfloat16)
    for k, out_ref in enumerate(cold_refs):
        span = slice(k * share, (k + 1) * share)
        out_ref[:, :width] = rows[span].astype(jnp.bfloat16)
        out_ref[:, width:] = (extra[span] + hot_extra).astype(jnp.bfloat16)


def route(me, request, table, tokens, stored, owners, share):
    count, width = tokens.shape
    packed = [(HOT_PARTS * share, width)] + [(share, width + EXTRA)] * owners
    outs = pl.pallas_call(
        functools.partial(route_kernel, stored, owners, share),
        out_shape=(
            *(jax.ShapeDtypeStruct(shape, jnp.bfloat16) for shape in packed),
            jax.ShapeDtypeStruct((1, count), jnp.int32),
            jax.ShapeDtypeStruct((1, 1), jnp.int32),
        ),
        in_specs=[scalars(), whole(), whole(), pl.BlockSpec(memory_space=pl.ANY)],
        out_specs=(whole(),) * (len(packed) + 2),
        scratch_shapes=[pltpu.VMEM((count, width), jnp.bfloat16), pltpu.SemaphoreType.DMA],
        compiler_params=params(ALL_VMEM),
    )(me, request.reshape(1, -1), table.reshape(1, -1), tokens)
    return outs[0], outs[1 : owners + 1], outs[-2], outs[-1]


def fetch_rows(source, target, sems):
    pieces = sems.shape[0]
    size = source.shape[0] // pieces
    copies = []
    for k in range(pieces):
        part = pl.ds(k * size, size)
        copies.append(pltpu.make_async_copy(source.at[part], target.at[part], sems.at[k]))
        copies[-1].start()
    return copies, size


def base_kernel(side_ref, tokens_ref, place_ref, weight_hbm, own_ref, other_ref, column_ref, weight, sems):
    half = own_ref.shape[1]
    copies, size = fetch_rows(weight_hbm, weight, sems)
    column_ref[...] = to_column(place_ref[...])
    total = None
    for k, copy in enumerate(copies):
        copy.wait()
        part = jnp.dot(
            tokens_ref[:, k * size : (k + 1) * size],
            weight[k * size : (k + 1) * size, :],
            preferred_element_type=jnp.float32,
        )
        total = part if total is None else total + part

    @pl.when(side_ref[0] == 0)
    def _():
        own_ref[...] = total[:, :half]
        other_ref[...] = total[:, half:]

    @pl.when(side_ref[0] != 0)
    def _():
        own_ref[...] = total[:, half:]
        other_ref[...] = total[:, :half]


def base_product(side, tokens, place, weight):
    column = jax.ShapeDtypeStruct((tokens.shape[0], 1), jnp.int32)
    half = jax.ShapeDtypeStruct((tokens.shape[0], weight.shape[1] // 2), jnp.float32)
    return pl.pallas_call(
        base_kernel,
        in_specs=[scalars(), whole(), whole(), pl.BlockSpec(memory_space=pltpu.HBM)],
        out_specs=(whole(),) * 3,
        out_shape=(half, half, column),
        scratch_shapes=[pltpu.VMEM(weight.shape, weight.dtype), pltpu.SemaphoreType.DMA((5,))],
        compiler_params=params(),
        cost_estimate=LITTLE,
    )(side, tokens, place, weight)


def keep_kernel(table_ref, out_ref, sem):
    copy = pltpu.make_async_copy(table_ref, out_ref, sem)
    copy.start()
    copy.wait()


def keep(table):
    return pl.pallas_call(
        keep_kernel,
        in_specs=[pl.BlockSpec(memory_space=pl.ANY)],
        out_specs=whole(),
        out_shape=pltpu.VMEM(table.shape, table.dtype),
        scratch_shapes=[pltpu.SemaphoreType.DMA],
        compiler_params=params(),
        cost_estimate=LITTLE,
    )(table)


def down_kernel(rank, blocks, guides, me_ref, *refs):
    guide_refs, refs = refs[:guides], refs[guides:]
    row_count = sum(1 for kind, _ in blocks if kind != COLD)
    rows_refs = list(refs[:row_count])
    weight_ref, out_ref, local_ref = refs[row_count:]
    width = weight_ref.shape[1]
    routing = [r[:, width:].astype(jnp.float32).T for r in guide_refs]
    local, rows = [], []
    for kind, guide in blocks:
        if kind == COLD:
            rows.append(guide_refs[guide][:, :width])
        else:
            rows.append(rows_refs.pop(0)[...])
        for k in {COLD: [0], HOT: range(2, 2 + 2 * HOT_PARTS, 2), REST: []}[kind]:
            mine = routing[guide][k : k + 1] == (me_ref[0] + 1).astype(jnp.float32)
            local.append(jnp.where(mine, routing[guide][k + 1 : k + 2], -1.0))
    local = jnp.concatenate(local, axis=1)
    rows = jnp.concatenate(rows, axis=0)
    block = 4 * rank
    out = jnp.zeros(out_ref.shape, jnp.float32)
    for first in range(0, weight_ref.shape[0], block):
        product = lax.dot_general(
            weight_ref[first : first + block, :],
            rows,
            (((1,), (1,)), ((), ())),
            preferred_element_type=jnp.float32,
        )
        for j in range(block // rank):
            mine = local == float(first // rank + j)
            out = out + jnp.where(mine, product[j * rank : (j + 1) * rank, :], 0.0)
    out_ref[...] = out
    local_ref[...] = local


def down(me, blocks, guides, row_arrays, table, rank):
    share = guides[0].shape[0]
    count = share * sum(kind == COLD for kind, _ in blocks) + sum(r.shape[0] for r in row_arrays)
    return pl.pallas_call(
        functools.partial(down_kernel, rank, blocks, len(guides)),
        in_specs=[scalars()] + [whole()] * (len(guides) + len(row_arrays) + 1),
        out_specs=(whole(), whole()),
        out_shape=(
            jax.ShapeDtypeStruct((rank, count), jnp.float32),
            jax.ShapeDtypeStruct((1, count), jnp.float32),
        ),
        compiler_params=params(),
        cost_estimate=LITTLE,
    )(me, *guides, *row_arrays, table)


def update(own_ref, other_ref, local_ref, weight_ref):
    rank, count = own_ref.shape
    pair = LANES // rank
    shrunk = (own_ref[...] + other_ref[...]).astype(jnp.bfloat16).astype(jnp.float32)
    doubled = jnp.concatenate([shrunk] * pair, axis=0).T
    local = jnp.broadcast_to(local_ref[...], (LANES, count)).T.astype(jnp.int32)
    lane_block = lax.broadcasted_iota(jnp.int32, (count, LANES), 1) // rank
    spread = jnp.concatenate(
        [
            jnp.where(lane_block + j * pair == local, doubled, 0.0).astype(jnp.bfloat16)
            for j in range(weight_ref.shape[0] // LANES)
        ],
        axis=1,
    )
    return jnp.dot(spread, weight_ref[...], preferred_element_type=jnp.float32)


def up_kernel(units, kept, to_ref, own_ref, other_ref, local_ref, weight_ref, *refs):
    out_ref, buffer, sems = refs[kept:]
    product = update(own_ref, other_ref, local_ref, weight_ref)
    share, features = buffer.shape[1:]
    copies = []
    for k, (place, column) in enumerate(units):
        buffer[k] = product[k * share : (k + 1) * share].astype(jnp.bfloat16)
        target = out_ref.at[to_ref[place], :, pl.ds(column * features, features)]
        copies.append(pltpu.make_async_copy(buffer.at[k], target, sems.at[k]))
        copies[-1].start()
    for copy in copies:
        copy.wait()


def up(targets, units, own, other, local, table, out):
    given = [] if isinstance(out, jax.ShapeDtypeStruct) else [out]
    anywhere = pl.BlockSpec(memory_space=pl.ANY)
    share = own.shape[1] // len(units)
    return pl.pallas_call(
        functools.partial(up_kernel, units, len(given)),
        in_specs=[scalars()] + [whole()] * 4 + [anywhere] * len(given),
        out_specs=anywhere,
        scratch_shapes=[
            pltpu.VMEM((len(units), share, table.shape[1]), jnp.bfloat16),
            pltpu.SemaphoreType.DMA((len(units),)),
        ],
        out_shape=jax.ShapeDtypeStruct(out.shape, jnp.bfloat16),
        input_output_aliases={5: 0} if given else {},
        compiler_params=params(),
        cost_estimate=LITTLE,
    )(targets, own, other, local, table, *given)


def finish_kernel(
    head, busy_ref, far_ref, own_ref, other_ref, back_ref, last_ref, place_ref, scale_ref, cos_ref, sin_ref, out_ref
):
    count, width = own_ref.shape
    owners, share, _ = back_ref.shape
    pieces = [back_ref[o, :, HOT_PARTS * width :].astype(jnp.float32) for o in range(owners)]
    from_far = busy_ref[0] == far_ref[0]
    for c in range(HOT_PARTS):
        columns = slice(c * width, (c + 1) * width)
        near = back_ref[busy_ref[0], :, columns].astype(jnp.float32)
        pieces.append(jnp.where(from_far, last_ref[0, :, columns].astype(jnp.float32), near))
    back = jnp.concatenate(pieces, axis=0).astype(jnp.bfloat16)
    chosen = place_ref[...] == lax.broadcasted_iota(jnp.int32, (count, back.shape[0]), 1)
    keys = (own_ref[...] + other_ref[...]) + jnp.dot(
        chosen.astype(jnp.float32).astype(jnp.bfloat16), back, preferred_element_type=jnp.float32
    )
    cosine = cos_ref[...]
    sine = sin_ref[...]
    for h in range(width // head):
        one = keys[:, h * head : (h + 1) * head]
        normed = (
            one
            * lax.rsqrt(jnp.mean(one * one, axis=-1, keepdims=True) + 1e-06)
            * scale_ref[...]
        )
        turned = pltpu.roll(normed, head // 2, 1)
        out_ref[:, h * head : (h + 1) * head] = (normed * cosine + turned * sine).astype(jnp.bfloat16)


def finish(busy, far, own, other, back, last, place, scale, cosine, sine):
    return pl.pallas_call(
        functools.partial(finish_kernel, scale.shape[0]),
        in_specs=[scalars()] * 2 + [whole()] * 8,
        out_specs=whole(),
        out_shape=jax.ShapeDtypeStruct(own.shape, jnp.bfloat16),
        compiler_params=params(),
    )(busy, far, own, other, back, last, place, scale.reshape(1, -1), cosine, sine)


def after(value, *earlier):
    return lax.optimization_barrier((value,) + earlier)[0]


def rope_tables(head, cached_token_length):
    half = head // 2
    inv_freq = rope_theta ** (-(jnp.arange(half, dtype=jnp.float32) * 2.0) / head)
    angles = cached_token_length.astype(jnp.float32)[:, None] * inv_freq[None, :]
    cosine = jnp.cos(angles)
    sine = jnp.sin(angles)
    return jnp.concatenate([cosine, cosine], axis=1), jnp.concatenate([-sine, sine], axis=1)


def swap(x):
    return lax.ppermute(x, "tensor", [(0, 1), (1, 0)])


def on_device(
    tokens,
    base_key_matrix,
    adapter_down_weight,
    adapter_up_weight,
    key_norm_scale,
    request_adapter,
    adapter_slot_table,
    cached_token_length,
):
    row_count, half_width = tokens.shape
    stored, rank, _ = adapter_down_weight.shape
    owners = lax.axis_size("dp")
    me = lax.axis_index("dp")
    side = lax.axis_index("tensor")
    share = (row_count + owners + 2) // (owners + 3)
    hot_count = HOT_PARTS * share
    down_table = adapter_down_weight.reshape(stored * rank, half_width)
    up_table = adapter_up_weight.reshape(stored * rank, -1)
    features = up_table.shape[1]

    here = me.reshape(1).astype(jnp.int32)
    hot, cold, place, busy = route(
        here, request_adapter, adapter_slot_table, tokens, stored, owners, share
    )

    ring = ring_order(owners)
    half_way = owners // 2

    def along(rows, distance):
        return lax.ppermute(
            rows, "dp", [(ring[i], ring[(i + distance) % owners]) for i in range(owners)]
        )

    distances = [0] + [d for s in range(1, half_way) for d in (s, -s)] + [half_way]
    sources = [[0] * (2 * owners) for _ in ring]
    for spot, index in enumerate(ring):
        sources[index] = [ring[(spot - d) % owners] for d in distances + list(range(owners))]
    order = lax.dynamic_index_in_dim(jnp.array(sources, jnp.int32), me, 0, keepdims=False)

    def product(blocks, rows):
        distances_of = sorted({d for _, d in blocks})
        blocks = [(kind, distances_of.index(d)) for kind, d in blocks]
        guides = lax.optimization_barrier((*(got[d] for d in distances_of), rows[0]))[:-1]
        own, local = down(here, blocks, list(guides), rows, down_table, rank)
        return own, swap(own), local

    group = [along(hot, 1), along(hot, -1)]
    waves = {d: [d, owners - d] for d in range(1, half_way)}
    waves[half_way - 1] = waves[half_way - 1] + [half_way]
    got = {0: cold[0]}
    for d in waves[1]:
        got[d] = along(cold[d], d)
    cut = hot_count // 2 // 16 * 16 if hot_count >= 32 else hot_count // 2

    def hot_units(first, blocks):
        return [(first + k, column) for k in range(blocks) for column in range(HOT_PARTS)]

    def cold_units(chosen):
        return [(owners + d, HOT_PARTS) for d in chosen]

    delta = jax.ShapeDtypeStruct((owners, share, (HOT_PARTS + 1) * features), jnp.bfloat16)
    down_table = keep(down_table)
    todo = [got[d] for d in waves[1]] + [down_table]
    for step in range(1, half_way):
        group = list(lax.optimization_barrier((*group, *todo))[:2])
        if step < half_way - 1:
            following = [along(group[0], 1), along(group[1], -1)]
            for d in waves[step + 1]:
                got[d] = along(after(cold[d], group[0]), d)
        else:
            following = [along(group[0][:cut], 1), along(group[1][cut:], -1)]
        rows, units = list(group), hot_units(2 * step - 1, 2)
        blocks = [(HOT, step), (HOT, owners - step)]
        if step == 1:
            rows, units, blocks = [hot] + rows, hot_units(0, 3), [(HOT, 0)] + blocks
        if step == half_way - 2:
            chosen = [d for d in range(owners) if d not in waves[half_way - 1]]
        elif step == half_way - 1:
            chosen = waves[step]
        else:
            chosen = []
        blocks += [(COLD, d) for d in chosen]
        delta = up(order, units + cold_units(chosen), *product(blocks, rows), up_table, delta)
        todo = [delta] + [got[d] for d in waves.get(step + 1, [])]
        group = following
    *group, delta = lax.optimization_barrier((*group, delta))
    back = lax.all_to_all(delta, "dp", split_axis=0, concat_axis=0, tiled=True)
    last = product([(HOT, half_way), (REST, half_way)], list(group))
    far_delta = jax.ShapeDtypeStruct((1, share, HOT_PARTS * features), jnp.bfloat16)
    far_delta = up(
        jnp.zeros((1,), jnp.int32), [(0, c) for c in range(HOT_PARTS)], *last, up_table, far_delta
    )
    tokens = after(tokens, far_delta)
    far_delta = along(far_delta, half_way)
    base_own, base_give, place = base_product(
        side.reshape(1).astype(jnp.int32), tokens, place, base_key_matrix
    )
    cosine, sine = rope_tables(key_norm_scale.shape[0], cached_token_length)
    return finish(
        busy.reshape(1),
        order[owners - 1 : owners],
        base_own,
        swap(base_give),
        back,
        far_delta,
        place,
        key_norm_scale,
        cosine,
        sine,
    )


def solution(mesh):
    placed = (
        P(("groups", "dp"), "tensor"),
        P("tensor", None),
        P(("groups", "dp"), None, "tensor"),
        P(("groups", "dp"), None, "tensor"),
        P(),
        P(("groups", "dp")),
        P("groups"),
        P(("groups", "dp")),
    )
    return jax.shard_map(
        on_device,
        mesh=mesh,
        in_specs=placed,
        out_specs=P(("groups", "dp"), "tensor"),
        check_vma=False,
    )
```

```python
import functools

import jax
import jax.numpy as jnp
from jax import lax
from jax.experimental import pallas as pl
from jax.experimental.pallas import tpu as pltpu
from jax.sharding import PartitionSpec as P

rope_theta = 1000000.0
LANES = 128
EXTRA = 128
COLD, HOT, REST = 0, 1, 2
HOT_PARTS = 3
ALL_VMEM = 60 * 1024 * 1024
LITTLE = pl.CostEstimate(flops=1, bytes_accessed=1, transcendentals=0)
SOME_VMEM = 32 * 1024 * 1024


def whole():
    return pl.BlockSpec(memory_space=pltpu.VMEM)


def scalars():
    return pl.BlockSpec(memory_space=pltpu.SMEM)


def params(limit=SOME_VMEM):
    return pltpu.CompilerParams(vmem_limit_bytes=limit)


def ring_order(owners):
    return [i for i in range(0, owners, 2)] + [i for i in range(owners - 1, 0, -2)]


def to_column(row):
    count = row.shape[1]
    square = lax.broadcasted_iota(jnp.int32, (count, count), 0) == lax.broadcasted_iota(
        jnp.int32, (count, count), 1
    )
    return jnp.sum(jnp.where(square, row, 0), axis=1, keepdims=True)


def spot_of(index, owners):
    return jnp.where(index % 2 == 0, index // 2, owners - 1 - index // 2)


def route_kernel(stored, owners, share, me_ref, request_ref, table_ref, tokens_hbm, hot_ref, *refs):
    cold_refs = refs[:owners]
    place_ref, busy_ref, tokens_ref, sem = refs[owners:]
    fetch = pltpu.make_async_copy(tokens_hbm, tokens_ref, sem)
    fetch.start()
    count = request_ref.shape[1]
    adapters = table_ref.shape[1]
    table_col = to_column(table_ref[...])
    match = request_ref[...] == lax.broadcasted_iota(jnp.int32, (adapters, count), 0)
    slot_row = jnp.sum(jnp.where(match, table_col, 0), axis=0, keepdims=True)
    slot_col = to_column(slot_row)
    owner_col = slot_col // stored
    owner_row = slot_row // stored
    row_id = lax.broadcasted_iota(jnp.int32, (count, count), 0)
    col_id = lax.broadcasted_iota(jnp.int32, (count, count), 1)
    earlier = (owner_col == owner_row) & (row_id < col_id)
    rank_row = jnp.sum(jnp.where(earlier, 1, 0), axis=0, keepdims=True)
    cold_total = owners * share
    place_ref[...] = jnp.where(
        rank_row < share, owner_row * share + rank_row, cold_total + rank_row - share
    )
    busy_ref[...] = jnp.max(jnp.where(rank_row >= share, owner_row, 0), axis=1, keepdims=True)
    distance = (spot_of(owner_row, owners) - spot_of(me_ref[0], owners) + owners) % owners
    position = jnp.where(rank_row < share, distance * share, cold_total - share) + rank_row
    total = cold_total + hot_ref.shape[0]
    pick = position == lax.broadcasted_iota(jnp.int32, (total, count), 0)
    pick = pick.astype(jnp.float32).astype(jnp.bfloat16)
    lane = lax.broadcasted_iota(jnp.int32, (count, EXTRA), 1)
    local_col = slot_col - owner_col * stored

    def beside(pick, first):
        codes = jnp.where(lane == first, owner_col + 1, jnp.where(lane == first + 1, local_col, 0))
        codes = codes.astype(jnp.float32).astype(jnp.bfloat16)
        return jnp.dot(pick, codes, preferred_element_type=jnp.float32)

    hot_extra = jnp.zeros((share, EXTRA), jnp.float32)
    for part in range(HOT_PARTS):
        piece = position - (cold_total + part * share) == lax.broadcasted_iota(
            jnp.int32, (share, count), 0
        )
        hot_extra = hot_extra + beside(piece.astype(jnp.float32).astype(jnp.bfloat16), 2 + 2 * part)
    width = tokens_ref.shape[1]
    extra = beside(pick, 0)
    fetch.wait()
    rows = jnp.dot(pick, tokens_ref[...], preferred_element_type=jnp.float32)
    hot_ref[...] = rows[cold_total:].astype(jnp.bfloat16)
    for k, out_ref in enumerate(cold_refs):
        span = slice(k * share, (k + 1) * share)
        out_ref[:, :width] = rows[span].astype(jnp.bfloat16)
        out_ref[:, width:] = (extra[span] + hot_extra).astype(jnp.bfloat16)


def route(me, request, table, tokens, stored, owners, share):
    count, width = tokens.shape
    packed = [(HOT_PARTS * share, width)] + [(share, width + EXTRA)] * owners
    outs = pl.pallas_call(
        functools.partial(route_kernel, stored, owners, share),
        out_shape=(
            *(jax.ShapeDtypeStruct(shape, jnp.bfloat16) for shape in packed),
            jax.ShapeDtypeStruct((1, count), jnp.int32),
            jax.ShapeDtypeStruct((1, 1), jnp.int32),
        ),
        in_specs=[scalars(), whole(), whole(), pl.BlockSpec(memory_space=pl.ANY)],
        out_specs=(whole(),) * (len(packed) + 2),
        scratch_shapes=[pltpu.VMEM((count, width), jnp.bfloat16), pltpu.SemaphoreType.DMA],
        compiler_params=params(ALL_VMEM),
    )(me, request.reshape(1, -1), table.reshape(1, -1), tokens)
    return outs[0], outs[1 : owners + 1], outs[-2], outs[-1]


def fetch_rows(source, target, sems):
    pieces = sems.shape[0]
    size = source.shape[0] // pieces
    copies = []
    for k in range(pieces):
        part = pl.ds(k * size, size)
        copies.append(pltpu.make_async_copy(source.at[part], target.at[part], sems.at[k]))
        copies[-1].start()
    return copies, size


def base_kernel(side_ref, tokens_ref, place_ref, weight_hbm, own_ref, other_ref, chosen_ref, weight, sems):
    half = own_ref.shape[1]
    copies, size = fetch_rows(weight_hbm, weight, sems)
    chosen = to_column(place_ref[...]) == lax.broadcasted_iota(jnp.int32, chosen_ref.shape, 1)
    chosen_ref[...] = chosen.astype(jnp.float32).astype(jnp.bfloat16)
    total = None
    for k, copy in enumerate(copies):
        copy.wait()
        part = jnp.dot(
            tokens_ref[:, k * size : (k + 1) * size],
            weight[k * size : (k + 1) * size, :],
            preferred_element_type=jnp.float32,
        )
        total = part if total is None else total + part

    @pl.when(side_ref[0] == 0)
    def _():
        own_ref[...] = total[:, :half]
        other_ref[...] = total[:, half:]

    @pl.when(side_ref[0] != 0)
    def _():
        own_ref[...] = total[:, half:]
        other_ref[...] = total[:, :half]


def base_product(side, tokens, place, places, weight):
    chosen = jax.ShapeDtypeStruct((tokens.shape[0], places), jnp.bfloat16)
    half = jax.ShapeDtypeStruct((tokens.shape[0], weight.shape[1] // 2), jnp.float32)
    return pl.pallas_call(
        base_kernel,
        in_specs=[scalars(), whole(), whole(), pl.BlockSpec(memory_space=pltpu.HBM)],
        out_specs=(whole(),) * 3,
        out_shape=(half, half, chosen),
        scratch_shapes=[pltpu.VMEM(weight.shape, weight.dtype), pltpu.SemaphoreType.DMA((5,))],
        compiler_params=params(),
        cost_estimate=LITTLE,
    )(side, tokens, place, weight)


def keep_kernel(table_ref, out_ref, sem):
    copy = pltpu.make_async_copy(table_ref, out_ref, sem)
    copy.start()
    copy.wait()


def keep(table):
    return pl.pallas_call(
        keep_kernel,
        in_specs=[pl.BlockSpec(memory_space=pl.ANY)],
        out_specs=whole(),
        out_shape=pltpu.VMEM(table.shape, table.dtype),
        scratch_shapes=[pltpu.SemaphoreType.DMA],
        compiler_params=params(),
        cost_estimate=LITTLE,
    )(table)


def down_kernel(rank, blocks, guides, me_ref, *refs):
    guide_refs, refs = refs[:guides], refs[guides:]
    row_count = sum(1 for kind, _ in blocks if kind != COLD)
    rows_refs = list(refs[:row_count])
    weight_ref, out_ref, local_ref = refs[row_count:]
    width = weight_ref.shape[1]
    routing = [r[:, width:].astype(jnp.float32).T for r in guide_refs]
    local, rows = [], []
    for kind, guide in blocks:
        if kind == COLD:
            rows.append(guide_refs[guide][:, :width])
        else:
            rows.append(rows_refs.pop(0)[...])
        for k in {COLD: [0], HOT: range(2, 2 + 2 * HOT_PARTS, 2), REST: []}[kind]:
            mine = routing[guide][k : k + 1] == (me_ref[0] + 1).astype(jnp.float32)
            local.append(jnp.where(mine, routing[guide][k + 1 : k + 2], -1.0))
    local = jnp.concatenate(local, axis=1)
    rows = jnp.concatenate(rows, axis=0)
    block = 4 * rank
    out = jnp.zeros(out_ref.shape, jnp.float32)
    for first in range(0, weight_ref.shape[0], block):
        product = lax.dot_general(
            weight_ref[first : first + block, :],
            rows,
            (((1,), (1,)), ((), ())),
            preferred_element_type=jnp.float32,
        )
        for j in range(block // rank):
            mine = local == float(first // rank + j)
            out = out + jnp.where(mine, product[j * rank : (j + 1) * rank, :], 0.0)
    out_ref[...] = out
    local_ref[...] = local


def down(me, blocks, guides, row_arrays, table, rank):
    share = guides[0].shape[0]
    count = share * sum(kind == COLD for kind, _ in blocks) + sum(r.shape[0] for r in row_arrays)
    return pl.pallas_call(
        functools.partial(down_kernel, rank, blocks, len(guides)),
        in_specs=[scalars()] + [whole()] * (len(guides) + len(row_arrays) + 1),
        out_specs=(whole(), whole()),
        out_shape=(
            jax.ShapeDtypeStruct((rank, count), jnp.float32),
            jax.ShapeDtypeStruct((1, count), jnp.float32),
        ),
        compiler_params=params(),
        cost_estimate=LITTLE,
    )(me, *guides, *row_arrays, table)


def update(own_ref, other_ref, local_ref, weight_ref):
    rank, count = own_ref.shape
    pair = LANES // rank
    shrunk = (own_ref[...] + other_ref[...]).astype(jnp.bfloat16).astype(jnp.float32)
    doubled = jnp.concatenate([shrunk] * pair, axis=0).T
    local = jnp.broadcast_to(local_ref[...], (LANES, count)).T.astype(jnp.int32)
    lane_block = lax.broadcasted_iota(jnp.int32, (count, LANES), 1) // rank
    spread = jnp.concatenate(
        [
            jnp.where(lane_block + j * pair == local, doubled, 0.0).astype(jnp.bfloat16)
            for j in range(weight_ref.shape[0] // LANES)
        ],
        axis=1,
    )
    return jnp.dot(spread, weight_ref[...], preferred_element_type=jnp.float32)


def up_kernel(units, kept, to_ref, own_ref, other_ref, local_ref, weight_ref, *refs):
    out_ref, buffer, sems = refs[kept:]
    product = update(own_ref, other_ref, local_ref, weight_ref)
    share, features = buffer.shape[1:]
    copies = []
    for k, (place, column) in enumerate(units):
        buffer[k] = product[k * share : (k + 1) * share].astype(jnp.bfloat16)
        target = out_ref.at[to_ref[place], :, pl.ds(column * features, features)]
        copies.append(pltpu.make_async_copy(buffer.at[k], target, sems.at[k]))
        copies[-1].start()
    for copy in copies:
        copy.wait()


def up(targets, units, own, other, local, table, out):
    given = [] if isinstance(out, jax.ShapeDtypeStruct) else [out]
    anywhere = pl.BlockSpec(memory_space=pl.ANY)
    share = own.shape[1] // len(units)
    return pl.pallas_call(
        functools.partial(up_kernel, units, len(given)),
        in_specs=[scalars()] + [whole()] * 4 + [anywhere] * len(given),
        out_specs=anywhere,
        scratch_shapes=[
            pltpu.VMEM((len(units), share, table.shape[1]), jnp.bfloat16),
            pltpu.SemaphoreType.DMA((len(units),)),
        ],
        out_shape=jax.ShapeDtypeStruct(out.shape, jnp.bfloat16),
        input_output_aliases={5: 0} if given else {},
        compiler_params=params(),
        cost_estimate=LITTLE,
    )(targets, own, other, local, table, *given)


def finish_kernel(
    head, busy_ref, far_ref, base_ref, back_ref, last_ref, chosen_ref, scale_ref, cos_ref, sin_ref, out_ref
):
    width = base_ref.shape[1]
    owners, share, _ = back_ref.shape
    pieces = [back_ref[o, :, HOT_PARTS * width :].astype(jnp.float32) for o in range(owners)]
    from_far = busy_ref[0] == far_ref[0]
    for c in range(HOT_PARTS):
        columns = slice(c * width, (c + 1) * width)
        near = back_ref[busy_ref[0], :, columns].astype(jnp.float32)
        pieces.append(jnp.where(from_far, last_ref[0, :, columns].astype(jnp.float32), near))
    back = jnp.concatenate(pieces, axis=0).astype(jnp.bfloat16)
    keys = base_ref[...] + jnp.dot(chosen_ref[...], back, preferred_element_type=jnp.float32)
    cosine = cos_ref[...]
    sine = sin_ref[...]
    for h in range(width // head):
        one = keys[:, h * head : (h + 1) * head]
        normed = (
            one
            * lax.rsqrt(jnp.mean(one * one, axis=-1, keepdims=True) + 1e-06)
            * scale_ref[...]
        )
        turned = pltpu.roll(normed, head // 2, 1)
        out_ref[:, h * head : (h + 1) * head] = (normed * cosine + turned * sine).astype(jnp.bfloat16)


def finish(busy, far, base, back, last, chosen, scale, cosine, sine):
    return pl.pallas_call(
        functools.partial(finish_kernel, scale.shape[0]),
        in_specs=[scalars()] * 2 + [whole()] * 7,
        out_specs=whole(),
        out_shape=jax.ShapeDtypeStruct(base.shape, jnp.bfloat16),
        compiler_params=params(),
    )(busy, far, base, back, last, chosen, scale.reshape(1, -1), cosine, sine)


def after(value, *earlier):
    return lax.optimization_barrier((value,) + earlier)[0]


def rope_tables(head, cached_token_length):
    half = head // 2
    inv_freq = rope_theta ** (-(jnp.arange(half, dtype=jnp.float32) * 2.0) / head)
    angles = cached_token_length.astype(jnp.float32)[:, None] * inv_freq[None, :]
    cosine = jnp.cos(angles)
    sine = jnp.sin(angles)
    return jnp.concatenate([cosine, cosine], axis=1), jnp.concatenate([-sine, sine], axis=1)


def swap(x):
    return lax.ppermute(x, "tensor", [(0, 1), (1, 0)])


def on_device(
    tokens,
    base_key_matrix,
    adapter_down_weight,
    adapter_up_weight,
    key_norm_scale,
    request_adapter,
    adapter_slot_table,
    cached_token_length,
):
    row_count, half_width = tokens.shape
    stored, rank, _ = adapter_down_weight.shape
    owners = lax.axis_size("dp")
    me = lax.axis_index("dp")
    side = lax.axis_index("tensor")
    share = (row_count + owners + 2) // (owners + 3)
    hot_count = HOT_PARTS * share
    down_table = adapter_down_weight.reshape(stored * rank, half_width)
    up_table = adapter_up_weight.reshape(stored * rank, -1)
    features = up_table.shape[1]

    here = me.reshape(1).astype(jnp.int32)
    hot, cold, place, busy = route(
        here, request_adapter, adapter_slot_table, tokens, stored, owners, share
    )

    ring = ring_order(owners)
    half_way = owners // 2

    def along(rows, distance):
        return lax.ppermute(
            rows, "dp", [(ring[i], ring[(i + distance) % owners]) for i in range(owners)]
        )

    distances = [0] + [d for s in range(1, half_way) for d in (s, -s)] + [half_way]
    sources = [[0] * (2 * owners) for _ in ring]
    for spot, index in enumerate(ring):
        sources[index] = [ring[(spot - d) % owners] for d in distances + list(range(owners))]
    order = lax.dynamic_index_in_dim(jnp.array(sources, jnp.int32), me, 0, keepdims=False)

    def product(blocks, rows):
        distances_of = sorted({d for _, d in blocks})
        blocks = [(kind, distances_of.index(d)) for kind, d in blocks]
        guides = lax.optimization_barrier((*(got[d] for d in distances_of), rows[0]))[:-1]
        own, local = down(here, blocks, list(guides), rows, down_table, rank)
        return own, swap(own), local

    group = [along(hot, 1), along(hot, -1)]
    waves = {d: [d, owners - d] for d in range(1, half_way)}
    waves[half_way - 1] = waves[half_way - 1] + [half_way]
    got = {0: cold[0]}
    for d in waves[1]:
        got[d] = along(cold[d], d)
    first_hot = owners * share
    cut = hot_count // 2 // 16 * 16 if hot_count >= 32 else hot_count // 2

    def hot_units(first, blocks):
        return [(first + k, column) for k in range(blocks) for column in range(HOT_PARTS)]

    def cold_units(chosen):
        return [(owners + d, HOT_PARTS) for d in chosen]

    delta = jax.ShapeDtypeStruct((owners, share, (HOT_PARTS + 1) * features), jnp.bfloat16)
    down_table = keep(down_table)
    todo = [got[d] for d in waves[1]] + [down_table]
    for step in range(1, half_way):
        group = list(lax.optimization_barrier((*group, *todo))[:2])
        if step < half_way - 1:
            following = [along(group[0], 1), along(group[1], -1)]
            for d in waves[step + 1]:
                got[d] = along(after(cold[d], group[0]), d)
        else:
            following = [along(group[0][:cut], 1), along(group[1][cut:], -1)]
        rows, units = list(group), hot_units(2 * step - 1, 2)
        blocks = [(HOT, step), (HOT, owners - step)]
        if step == 1:
            rows, units, blocks = [hot] + rows, hot_units(0, 3), [(HOT, 0)] + blocks
        if step == half_way - 2:
            chosen = [d for d in range(owners) if d not in waves[half_way - 1]]
        elif step == half_way - 1:
            chosen = waves[step]
        else:
            chosen = []
        blocks += [(COLD, d) for d in chosen]
        delta = up(order, units + cold_units(chosen), *product(blocks, rows), up_table, delta)
        todo = [delta] + [got[d] for d in waves.get(step + 1, [])]
        group = following
    delta = after(delta, *group)
    back = lax.all_to_all(delta, "dp", split_axis=0, concat_axis=0, tiled=True)
    last = product([(HOT, half_way), (REST, half_way)], list(group))
    far_delta = jax.ShapeDtypeStruct((1, share, HOT_PARTS * features), jnp.bfloat16)
    far_delta = up(
        jnp.zeros((1,), jnp.int32), [(0, c) for c in range(HOT_PARTS)], *last, up_table, far_delta
    )
    tokens = after(tokens, far_delta)
    far_delta = along(far_delta, half_way)
    base_own, base_give, chosen = base_product(
        side.reshape(1).astype(jnp.int32), tokens, place, first_hot + hot_count, base_key_matrix
    )
    cosine, sine = rope_tables(key_norm_scale.shape[0], cached_token_length)
    return finish(
        busy.reshape(1),
        order[owners - 1 : owners],
        base_own + swap(base_give),
        back,
        far_delta,
        chosen,
        key_norm_scale,
        cosine,
        sine,
    )


def solution(mesh):
    placed = (
        P(("groups", "dp"), "tensor"),
        P("tensor", None),
        P(("groups", "dp"), None, "tensor"),
        P(("groups", "dp"), None, "tensor"),
        P(),
        P(("groups", "dp")),
        P("groups"),
        P(("groups", "dp")),
    )
    return jax.shard_map(
        on_device,
        mesh=mesh,
        in_specs=placed,
        out_specs=P(("groups", "dp"), "tensor"),
        check_vma=False,
    )
```
